1024 devices in a mesh: row: 64 (over x_hi, z), col: 16 (over y, x_lo, core).
Axes of the slice: x: 4 (x_hi: 2, x_lo: 2; x = x_hi * 2 + x_lo), y: 4, z: 32, core: 2. Of those that a mesh axis runs over, the one named last changes fastest.
Arguments:
- features: bfloat16 [131072, 128], P('col'), may hold values from -6 to 6
- source_degree: int32 [131072], P('col'), may hold values from 1 to 31
- tile_coords: int32 [64, 16, 2, 96], P('row', 'col'), may hold values from 0 to 127, as said below
- tile_counts: int32 [64, 16, 96], P('row', 'col'), may hold values from 0 to 96, as said below
- tile_values: bfloat16 [64, 16, 96, 4096], P('row', 'col'), may hold values from 0 to 1.5, as said below
- weight: bfloat16 [128, 128], replicated, may hold values from -0.5 to 0.5
- node_order: int32 [1024, 128], P(('row', 'col')), may hold values from 0 to 127, each once within a row
- cotangent: bfloat16 [131072, 128], P(('row', 'col')), may hold values from -24 to 24
Outputs:
- activations: bfloat16 [131072, 128], P(('row', 'col'))
- weight_grad: float32 [128, 128], replicated
The draws below stay inside these ranges and needn't reach their ends.
Inputs may be any that keep to these rules, and one draw needn't show every extreme that they name: `tile_coords`: tile rows lie below 32, tile columns below 128; some slot reaches each end. `tile_counts`: within each group of 24 slots of one offset the nonempty slots come first; every group has at least one nonempty and one empty slot. `tile_values`: each tile has exactly as many nonzero entries as its slot's count, each between 0.5 and 1.5.
All inputs are finite; a program needn't handle non-finite values.
Results may differ from the reference program's by a relative error of at most 0.0057.
Values may be sent and summed in bfloat16 or wider, within the bound.
No kernel may reach another device: no remote copies, remote signals or barrier semaphores. Data moves between devices by JAX's collectives and lax.ppermute only.
A program may use at most 64 MiB of HBM per device.

```python
import jax
import jax.numpy as jnp
from jax import lax

F = 128
TB = 64
OUT_DEV = 128
TPS = 24
STEPS = 4
TILES = 96
RP = 2048
RT = 32
CT = 128
NODES = 131072
N_ROW = 64
N_COL = 16


def shared_counts(key):
    key = jax.random.fold_in(key, 23)
    first, second = jax.random.split(key)
    filled = jax.random.randint(first, (N_ROW, N_COL, STEPS, 1), TPS // 2, TPS)
    filled = jnp.maximum(filled, 1)
    slot = jnp.arange(TPS)[None, None, None, :]
    column = jnp.arange(N_COL)[None, :, None, None]
    ceiling = TB // 2 + TB * column // max(N_COL - 1, 1)
    counts = jax.random.randint(second, (N_ROW, N_COL, STEPS, TPS), 0, 1 << 20) % ceiling + 1
    counts = jnp.where(slot == 0, ceiling, counts)
    counts = jnp.where(slot < filled, counts, 0)
    return counts.reshape(N_ROW, N_COL, TILES).astype(jnp.int32)


def draw_tile_coords(key, part):
    key = jax.random.fold_in(key, 11)
    first, second = jax.random.split(key)
    rows = jax.random.randint(first, (N_ROW, N_COL, 1, TILES), 0, RT)
    cols = jax.random.randint(second, (N_ROW, N_COL, 1, TILES), 0, CT)
    rows = rows.at[:, :, :, 1].set(RT - 1)
    cols = cols.at[:, :, :, 0].set(CT - 1)
    return jnp.concatenate([rows, cols], axis=2).astype(jnp.int32)


def draw_tile_counts(key, part):
    counts = shared_counts(key)
    return counts


def draw_tile_values(key, part):
    counts = shared_counts(key)
    key = jax.random.fold_in(key, 37)
    keys = jax.random.split(key, 6)
    cells = TB * TB
    lead = (N_ROW, N_COL, TILES, 1)
    mult_one = jax.random.randint(keys[0], lead, 0, cells // 2) * 2 + 1
    add_one = jax.random.randint(keys[1], lead, 0, cells)
    mask_one = jax.random.randint(keys[2], lead, 0, cells)
    mult_two = jax.random.randint(keys[3], lead, 0, cells // 2) * 2 + 1
    add_two = jax.random.randint(keys[4], lead, 0, cells)
    position = jnp.arange(cells)[None, None, None, :]
    rank = (mult_one * position + add_one) % cells
    rank = jnp.bitwise_xor(rank, mask_one)
    rank = (mult_two * rank + add_two) % cells
    weights = jax.random.uniform(keys[5], (N_ROW, N_COL, TILES, cells), jnp.float32, 0.5, 1.5)
    values = jnp.where(rank < counts[..., None], weights, 0.0)
    return values.astype(jnp.bfloat16)


def with_ends(drawn, key, smallest, high):
    place = [jax.random.randint(jax.random.fold_in(key, axis), (), 0, length) for axis, length in enumerate(drawn.shape)]
    main_axis = drawn.shape.index(max(drawn.shape))
    neighbour = place[:main_axis] + [(place[main_axis] + 1) % drawn.shape[main_axis]] + place[main_axis + 1:]
    return drawn.at[tuple(place)].set(smallest).at[tuple(neighbour)].set(high)


def strengthened(result, rng, source, target, parts, factor):
    owner, partner = [(jnp.arange(result.shape[dim]) // (result.shape[dim] // parts)).reshape([-1 if axis == dim else 1 for axis in range(result.ndim)]) for dim in (source, target)]
    chosen = jax.random.permutation(rng, parts)[partner]
    strong = (owner == chosen) | (owner == (partner + parts // 2) % parts)
    return jnp.where(strong, factor * result, result)


def level_of(key, shape, shards, least, top_value):
    level, own = 1.0, jax.random.fold_in(key, 6)
    for dim, parts in shards:
        draws = jnp.exp(jax.random.uniform(jax.random.fold_in(own, dim), (parts,), jnp.float32, least / len(shards), top_value / len(shards)))
        level = level * jnp.repeat(draws, shape[dim] // parts).reshape([-1 if axis == dim else 1 for axis in range(len(shape))])
    return level


def bell_draw(rng, shape, deviation, limit, pieces=(), held_as=jnp.bfloat16):
    array = deviation * jax.random.normal(rng, shape, jnp.float32)
    if pieces:
        array = array * level_of(rng, shape, pieces, -0.22, 0.18)
    return jnp.clip(array, -limit, limit).astype(held_as)


def heavy_noise(own_key, extent, width, most, cuts, heavy, dtype=jnp.bfloat16):
    array = width * jax.random.normal(own_key, extent, jnp.float32)
    if cuts:
        array = array * level_of(own_key, extent, cuts, -0.22, 0.18)
    return jnp.clip(strengthened(array, jax.random.fold_in(own_key, 3), *heavy), -most, most).astype(dtype)


def setup_inputs(seed: int = 0) -> dict:
    seeds = jax.random.split(jax.random.key(seed), 9)
    features = bell_draw(seeds[0], (NODES, F), 1.0, 6.0, ((0, 16),))
    source_degree = with_ends(jax.random.randint(seeds[1], (NODES,), 1, 32), jax.random.fold_in(seeds[1], 1), 1, 31).astype(jnp.int32)
    tile_coords = draw_tile_coords(jax.random.fold_in(seeds[8], 71), 0)
    tile_counts = draw_tile_counts(jax.random.fold_in(seeds[8], 71), 0)
    tile_values = draw_tile_values(jax.random.fold_in(seeds[8], 71), 0)
    weight = bell_draw(seeds[5], (F, F), F ** -0.5, 0.5)
    node_order = jax.vmap(lambda own: jax.random.permutation(own, OUT_DEV))(jax.random.split(seeds[6], (N_ROW * N_COL))).reshape((N_ROW * N_COL, OUT_DEV)).astype(jnp.int32)
    cotangent = heavy_noise(seeds[7], (NODES, F), 1.0, 24.0, ((0, 1024),), (0, 1, 128, 5.5))
    return dict(features=features, source_degree=source_degree, tile_coords=tile_coords, tile_counts=tile_counts, tile_values=tile_values, weight=weight, node_order=node_order, cotangent=cotangent)


def reference(features, source_degree, tile_coords, tile_counts, tile_values, weight, node_order, cotangent):
    scaled = (features.astype(jnp.float32) * lax.rsqrt(1.0 + source_degree.astype(jnp.float32))[:, None]).astype(jnp.bfloat16)
    panels = scaled.reshape(N_COL, CT, TB, F).astype(jnp.float32)
    slot_step = (jnp.arange(TILES) // TPS).astype(jnp.int32)
    col_pos = jnp.arange(N_COL).astype(jnp.int32)
    source = ((col_pos[:, None] - slot_step[None, :]) % N_COL).astype(jnp.int32)

    def one_row(inputs):
        coords, counts, values = inputs
        blocks = panels[source, coords[:, 1]]
        occupied = (counts > 0).astype(jnp.float32)
        squares = values.reshape(N_COL, TILES, TB, TB).astype(jnp.float32)
        products = jnp.einsum('ctij,ctjf->ctif', squares, blocks, precision=lax.Precision.HIGHEST) * occupied[:, :, None, None]
        row_weights = lax.optimization_barrier(jnp.sum(squares, axis=-1)) * occupied[:, :, None]
        targets = coords[:, 0].reshape(-1)
        summed = jnp.zeros((RT, TB, F), jnp.float32).at[targets].add(products.reshape(-1, TB, F))
        degree = jnp.zeros((RT, TB), jnp.float32).at[targets].add(row_weights.reshape(-1, TB))
        return (summed.reshape(RP, F), degree.reshape(RP))
    sums, degrees = lax.map(one_row, (tile_coords, tile_counts, tile_values))
    sums = sums.reshape(NODES, F) + scaled.astype(jnp.float32)
    degrees = degrees.reshape(NODES)
    normed = (sums * lax.rsqrt(1.0 + degrees)[:, None]).astype(jnp.bfloat16)
    act = jnp.maximum(jnp.dot(normed, weight, preferred_element_type=jnp.float32), 0.0).astype(jnp.bfloat16)
    offsets = (jnp.arange(N_ROW * N_COL) * OUT_DEV).astype(jnp.int32)
    flat = (node_order + offsets[:, None]).reshape(-1)
    activations = act[flat]
    weight_grad = jnp.dot(normed[flat].T, cotangent, preferred_element_type=jnp.float32) * NODES ** (-0.5)
    return (activations, weight_grad)
```

```python
import jax
import jax.numpy as jnp
from jax import lax
from jax.sharding import PartitionSpec as P

TB = 64
META_ROWS = 16


def passed_along(value, axis, steps):
    count = lax.axis_size(axis)
    pairs = [(source, (source + steps) % count) for source in range(count)]
    return lax.ppermute(value, axis, pairs)


def three_parts(value):
    high = value.astype(jnp.bfloat16)
    rest = value - high.astype(jnp.float32)
    middle = rest.astype(jnp.bfloat16)
    low = (rest - middle.astype(jnp.float32)).astype(jnp.bfloat16)
    return high, middle, low


def exchanged(parts, axis):
    return lax.all_to_all(parts, axis, 0, 0)


def to_all(value, axis):
    count = lax.axis_size(axis)
    copies = jnp.broadcast_to(value[None], (count, *value.shape))
    return exchanged(lax.optimization_barrier(copies), axis)


def per_device(
    features, source_degree, tile_coords, tile_counts, tile_values, weight, node_order, cotangent
):
    columns = lax.axis_size("col")
    row_count = lax.axis_size("row")
    step_total = min(4, columns)
    coords = tile_coords.reshape(2, step_total, -1)
    occupied = (tile_counts.reshape(step_total, -1) > 0).astype(jnp.bfloat16)
    per_step = coords.shape[-1]
    panel_rows, feat_dim = features.shape
    out_rows = node_order.shape[-1]
    row_panel = out_rows * columns
    row_tiles = row_panel // TB

    places = jnp.stack([coords[0].astype(jnp.bfloat16), coords[1].astype(jnp.bfloat16), occupied], axis=1)
    places = jnp.pad(places, ((0, 0), (0, META_ROWS - 3), (0, 128 - per_step)))
    packed = jnp.concatenate([tile_values.reshape(step_total, -1, 128), places], axis=1)
    packed = lax.optimization_barrier(packed)
    moved = [packed[0]] + [passed_along(packed[step], "col", -step) for step in range(1, step_total)]

    scaled = (
        features.astype(jnp.float32) * lax.rsqrt(1.0 + source_degree.astype(jnp.float32))[:, None]
    ).astype(jnp.bfloat16)
    panel_blocks = scaled.reshape(-1, TB, feat_dim)

    def one_step(group):
        place = group[-META_ROWS:, :per_step]
        tile_row, tile_col, filled = place[0], place[1].astype(jnp.int32), place[2]
        tiles = group[:-META_ROWS].reshape(per_step, TB, TB)
        targets = (
            tile_row.astype(jnp.int32)[None, :] == jnp.arange(row_tiles)[:, None]
        ).astype(jnp.float32) * filled.astype(jnp.float32)[None, :]
        products = jnp.einsum(
            "tij,tjf->tif", tiles, panel_blocks[tile_col], preferred_element_type=jnp.float32
        )
        sums = jnp.einsum("rt,tif->rif", targets, products, precision=lax.Precision.HIGHEST)
        weights = jnp.sum(tiles, axis=-1, dtype=jnp.float32)
        return sums, jnp.dot(targets, weights, precision=lax.Precision.HIGHEST)

    total, degree = one_step(moved[0])
    for group in moved[1:]:
        more, more_degree = one_step(group)
        total, degree = total + more, degree + more_degree
    row_index = lax.axis_index("row")
    owner = row_index * columns // row_count
    self_start = row_index * row_panel % panel_rows
    self_rows = lax.dynamic_slice_in_dim(scaled, self_start, row_panel, 0).astype(jnp.float32)
    holder = (lax.axis_index("col") == owner).astype(jnp.float32)
    partial_value = total.reshape(row_panel, feat_dim) + holder * self_rows
    degree_parts = jnp.stack(three_parts(degree.reshape(columns, out_rows)), axis=1)
    outgoing = jnp.concatenate(
        [
            partial_value.astype(jnp.bfloat16).reshape(columns, out_rows, feat_dim),
            jnp.pad(degree_parts, ((0, 0), (0, META_ROWS - 3), (0, 0))),
        ],
        axis=1,
    )
    arrived = exchanged(outgoing, "col").astype(jnp.float32).sum(0)
    sums = arrived[:out_rows]
    degrees = arrived[out_rows] + arrived[out_rows + 1] + arrived[out_rows + 2]
    normed = (sums * lax.rsqrt(1.0 + degrees)[:, None]).astype(jnp.bfloat16)
    order = node_order.reshape(-1)
    ordered = normed[order]
    activations = jnp.maximum(
        jnp.dot(ordered, weight, preferred_element_type=jnp.float32), 0.0
    ).astype(jnp.bfloat16)
    node_total = out_rows * row_count * columns
    local_grad = jnp.dot(ordered.T, cotangent, preferred_element_type=jnp.float32) * node_total ** (
        -0.5
    )
    share = exchanged(local_grad.reshape(columns, -1, feat_dim), "col").sum(0)
    share = to_all(share, "row").sum(0)
    weight_grad = to_all(share, "col").reshape(local_grad.shape)
    return (activations, weight_grad)


def solution(mesh):
    in_specs = (
        P("col", None),
        P("col"),
        P("row", "col", None, None),
        P("row", "col", None),
        P("row", "col", None, None),
        P(),
        P(("row", "col"), None),
        P(("row", "col"), None),
    )
    out_specs = (P(("row", "col"), None), P())
    return jax.shard_map(
        per_device, mesh=mesh, in_specs=in_specs, out_specs=out_specs, check_vma=False
    )
```

```python
import jax
import jax.numpy as jnp
from jax import lax
from jax.experimental import pallas as pl
from jax.experimental.pallas import tpu as pltpu
from jax.sharding import Mesh, PartitionSpec as P

TB = 64
HALF = TB // 2
META_ROWS = 16
UNROLL = 4
ROW = ("x_hi", "z")
PLANE = ("x_hi", "col")


def passed_along(value, axis, steps):
    count = lax.axis_size(axis)
    pairs = [(source, (source + steps) % count) for source in range(count)]
    return lax.ppermute(value, axis, pairs)


def exchanged(parts, axis):
    return lax.all_to_all(parts, axis, 0, 0)


def to_all(value, axis):
    count = lax.psum(1, axis)
    copies = jnp.broadcast_to(value[None], (count, *value.shape))
    return exchanged(lax.optimization_barrier(copies), axis)


def two_parts(value):
    high = value.astype(jnp.bfloat16)
    return high, (value - high.astype(jnp.float32)).astype(jnp.bfloat16)


def side_by_side(block):
    none = jnp.zeros_like(block)
    return jnp.concatenate(
        [jnp.concatenate([block, none], axis=1), jnp.concatenate([none, block], axis=1)], axis=0
    )


def tiles_kernel(place_ref, panel_ref, *refs):
    groups, out_ref, total = refs[:-2], refs[-2], refs[-1]
    tiles = (groups[0].shape[0] - META_ROWS) // HALF
    feat = panel_ref.shape[1]
    flags = len(groups) * 2 * tiles
    self_loop, self_start = place_ref[flags + len(groups)], place_ref[flags + len(groups) + 1]
    row_tiles = total.shape[0] // HALF

    total[...] = jnp.zeros_like(total)

    @pl.when(self_loop > 0)
    def _():
        at = lax.broadcasted_iota(jnp.int32, (HALF, 2 * TB), 1)
        row = lax.broadcasted_iota(jnp.int32, (HALF, 2 * TB), 0)
        same = (at % TB == 2 * row + at // TB).astype(jnp.float32).astype(jnp.bfloat16)

        @pl.loop(0, row_tiles // UNROLL)
        def _(first):
            for one in range(UNROLL):
                tile = first * UNROLL + one
                block = panel_ref[pl.ds(pl.multiple_of((self_start + tile) * TB, TB), TB), :]
                total[pl.ds(pl.multiple_of(tile * HALF, HALF), HALF), : 2 * feat] = jnp.dot(
                    same, side_by_side(block), preferred_element_type=jnp.float32
                )

    for index, group in enumerate(groups):

        @pl.loop(0, place_ref[flags + index])
        def _(first):
            for one in range(UNROLL):
                slot = first * UNROLL + one
                at = index * 2 * tiles + slot
                tile_row, tile_col = place_ref[at], place_ref[at + tiles]
                tile = group[pl.ds(pl.multiple_of(slot * HALF, HALF), HALF), :]
                block = panel_ref[pl.ds(pl.multiple_of(tile_col * TB, TB), TB), :]
                product = jnp.dot(tile, side_by_side(block), preferred_element_type=jnp.float32)
                rows = pl.ds(pl.multiple_of(tile_row * HALF, HALF), HALF)
                total[rows, : 2 * feat] += product
                total[rows, 2 * feat :] += tile.astype(jnp.float32)

    out_rows = total.shape[0] // out_ref.shape[0]
    lane = lax.broadcasted_iota(jnp.int32, (META_ROWS, 2 * TB), 1)
    line = lax.broadcasted_iota(jnp.int32, (META_ROWS, 2 * TB), 0)
    half = (lane // TB == line % 2).astype(jnp.float32).astype(jnp.bfloat16)
    part = lax.broadcasted_iota(jnp.int32, (META_ROWS, out_rows), 0) // 2

    @pl.loop(0, out_ref.shape[0])
    def _(device):
        rows = pl.ds(pl.multiple_of(device * out_rows, out_rows), out_rows)
        out_ref[device, :out_rows, :] = total[rows, : 2 * feat].astype(out_ref.dtype)
        degree = sum(
            lax.dot_general(
                half, piece, (((1,), (1,)), ((), ())), preferred_element_type=jnp.float32
            )
            for piece in two_parts(total[rows, 2 * feat :])
        )
        high, low = (piece.astype(jnp.float32) for piece in two_parts(degree))
        lines = jnp.where(part == 0, high, jnp.where(part == 1, low, 0.0))
        none = jnp.zeros((META_ROWS, out_ref.shape[2] - out_rows), jnp.float32)
        out_ref[device, out_rows:, :] = jnp.concatenate([lines, none], axis=1).astype(out_ref.dtype)


def layer_kernel(node_total, arrived_ref, order_ref, weight_ref, cotangent_ref, act_ref, grad_ref):
    lines = arrived_ref.shape[1] - META_ROWS
    nodes, feat = cotangent_ref.shape
    total = arrived_ref[0].astype(jnp.float32)
    for device in range(1, arrived_ref.shape[0]):
        total += arrived_ref[device].astype(jnp.float32)
    diagonal = lax.broadcasted_iota(jnp.int32, (lines, lines), 0) == lax.broadcasted_iota(
        jnp.int32, (lines, lines), 1
    )
    normed = []
    for half in range(2):
        degrees = total[lines + half : lines + half + 1, :lines]
        degrees += total[lines + half + 2 : lines + half + 3, :lines]
        scale = jnp.where(diagonal, lax.rsqrt(1.0 + degrees), 0.0).sum(axis=1, keepdims=True)
        normed.append(total[:lines, half * feat : (half + 1) * feat] * scale)
    normed = jnp.concatenate(normed, axis=0).astype(jnp.bfloat16)
    line = lax.broadcasted_iota(jnp.int32, (nodes, nodes), 0)
    node = 2 * (line % lines) + line // lines
    chosen = (order_ref[...] == node).astype(jnp.float32).astype(jnp.bfloat16)
    over_rows = (((0,), (0,)), ((), ()))
    ordered = lax.dot_general(
        chosen, normed, over_rows, preferred_element_type=jnp.float32
    ).astype(jnp.bfloat16)
    pre = jnp.dot(ordered, weight_ref[...], preferred_element_type=jnp.float32)
    act_ref[...] = jnp.maximum(pre, 0.0).astype(act_ref.dtype)
    grad_ref[...] = (
        lax.dot_general(
            ordered, cotangent_ref[...], over_rows, preferred_element_type=jnp.float32
        )
        * node_total ** (-0.5)
    )


def per_device(
    features, source_degree, tile_coords, tile_counts, tile_values, weight, node_order, cotangent
):
    columns = lax.axis_size("col")
    row_count = lax.psum(1, ROW)
    step_total = min(4, columns)
    coords = tile_coords.reshape(2, step_total, -1)
    occupied = tile_counts.reshape(step_total, -1) > 0
    per_step = coords.shape[-1]
    panel_rows, feat_dim = features.shape
    out_rows = node_order.shape[-1]
    row_panel = out_rows * columns
    vmem = pl.BlockSpec(memory_space=pltpu.VMEM)
    smem = pl.BlockSpec(memory_space=pltpu.SMEM)
    params = pltpu.CompilerParams(vmem_limit_bytes=32 * 1024 * 1024)

    filled = jnp.broadcast_to(occupied.sum(axis=1, keepdims=True), occupied.shape)
    places = jnp.stack([coords[0], coords[1], filled], axis=1).astype(jnp.bfloat16)
    places = jnp.pad(places, ((0, 0), (0, META_ROWS - 3), (0, 128 - per_step)))
    tiles = jnp.where(occupied[..., None], tile_values.reshape(step_total, per_step, -1), 0)
    packed = jnp.concatenate([tiles.reshape(step_total, -1, 128), places], axis=1)
    packed = lax.optimization_barrier(packed)
    groups = [packed[0]] + [
        passed_along(packed[step], "col", -step) for step in range(1, step_total)
    ]
    scaled = (
        features.astype(jnp.float32) * lax.rsqrt(1.0 + source_degree.astype(jnp.float32))[:, None]
    ).astype(jnp.bfloat16)
    row_index = lax.axis_index(ROW)
    holder = lax.axis_index("col") == row_index * columns // row_count
    self_start = row_index * row_panel % panel_rows // TB
    met = jnp.stack([group[-META_ROWS:] for group in groups]).astype(jnp.int32)
    place = jnp.concatenate(
        [
            met[:, :2, :per_step].reshape(-1),
            (met[:, 2, 0] + UNROLL - 1) // UNROLL,
            jnp.stack([holder.astype(jnp.int32), self_start.astype(jnp.int32)]),
        ]
    )
    lines = out_rows // 2
    outgoing = pl.pallas_call(
        tiles_kernel,
        out_shape=jax.ShapeDtypeStruct((columns, lines + META_ROWS, 2 * feat_dim), jnp.bfloat16),
        in_specs=[smem] + [vmem] * (1 + step_total),
        out_specs=vmem,
        scratch_shapes=[pltpu.VMEM((row_panel // 2, 2 * feat_dim + 2 * TB), jnp.float32)],
        compiler_params=params,
        name="tiles",
    )(place, scaled, *groups)
    arrived = exchanged(outgoing, "col")
    node_total = out_rows * row_count * columns
    activations, local_grad = pl.pallas_call(
        lambda *refs: layer_kernel(node_total, *refs),
        out_shape=(
            jax.ShapeDtypeStruct((out_rows, feat_dim), jnp.bfloat16),
            jax.ShapeDtypeStruct((feat_dim, feat_dim), jnp.float32),
        ),
        in_specs=[vmem] * 4,
        out_specs=(vmem, vmem),
        compiler_params=params,
        name="layer",
    )(arrived, node_order, weight, cotangent)
    share = exchanged(local_grad.reshape(lax.psum(1, PLANE), -1, feat_dim), PLANE).sum(0)
    share = to_all(share, "z").sum(0)
    weight_grad = to_all(share, PLANE).reshape(local_grad.shape)
    return (activations, weight_grad)


def solution(mesh):
    rows, columns = mesh.devices.shape
    apart = Mesh(mesh.devices.reshape(2, rows // 2, columns), (*ROW, "col"))
    both = (*ROW, "col")
    in_specs = (
        P("col", None),
        P("col"),
        P(ROW, "col", None, None),
        P(ROW, "col", None),
        P(ROW, "col", None, None),
        P(),
        P(both, None),
        P(both, None),
    )
    out_specs = (P(both, None), P())
    return jax.shard_map(
        per_device, mesh=apart, in_specs=in_specs, out_specs=out_specs, check_vma=False
    )
```

```python
import functools

import jax
import jax.numpy as jnp
from jax import lax
from jax.experimental import pallas as pl
from jax.experimental.pallas import tpu as pltpu
from jax.sharding import Mesh, PartitionSpec as P

TB = 64
HALF = TB // 2
LANES = 2 * TB
META_ROWS = 16
META_USED = 8
UNROLL = 6
SELF_UNROLL = 8
ROW = ("x_hi", "z")
PLANE = ("x_hi", "col")
VMEM = pl.BlockSpec(memory_space=pltpu.VMEM)
SMEM = pl.BlockSpec(memory_space=pltpu.SMEM)
PARAMS = pltpu.CompilerParams(vmem_limit_bytes=32 * 1024 * 1024)


def passed_along(value, axis, steps):
    count = lax.axis_size(axis)
    pairs = [(source, (source + steps) % count) for source in range(count)]
    return lax.ppermute(value, axis, pairs)


def exchanged(parts, axis):
    return lax.all_to_all(parts, axis, 0, 0)


def to_all(value, axis):
    count = lax.psum(1, axis)
    copies = jnp.broadcast_to(value[None], (count, *value.shape))
    return exchanged(lax.optimization_barrier(copies), axis)


def two_parts(value):
    high = value.astype(jnp.bfloat16)
    return high, (value - high.astype(jnp.float32)).astype(jnp.bfloat16)


def side_by_side(block):
    none = jnp.zeros_like(block)
    return jnp.concatenate(
        [jnp.concatenate([block, none], axis=1), jnp.concatenate([none, block], axis=1)], axis=0
    )


def pack_kernel(coords_ref, counts_ref, values_ref, *refs):
    groups, wide, meta = refs[:-2], refs[-2], refs[-1]
    tiles = values_ref.shape[0]
    for chunk in range(HALF):
        piece = values_ref[:, chunk * LANES : (chunk + 1) * LANES].astype(jnp.float32)
        wide[pl.ds(chunk, tiles, stride=HALF), :] = piece
    meta[...] = jnp.zeros_like(meta)
    meta[0:2, :tiles] = coords_ref[...].astype(jnp.float32)
    meta[2:3, :tiles] = counts_ref[...].astype(jnp.float32)
    rows = wide.shape[0] // len(groups)
    for index, group in enumerate(groups):
        group[:rows, :] = wide[index * rows : (index + 1) * rows, :].astype(group.dtype)
        group[rows:, :] = meta[...].astype(group.dtype)


def places(groups, first, per_group, staged, held, sem):
    lane = lax.broadcasted_iota(jnp.int32, (1, LANES), 1)
    for index, group in enumerate(groups):
        meta = group[group.shape[0] - META_ROWS :, :].astype(jnp.float32).astype(jnp.int32)
        start = (first + index) * per_group
        own = (lane >= start) & (lane < start + per_group) & (meta[2:3, :] > 0)
        filled = own.astype(jnp.int32).astype(jnp.float32).sum(axis=1, keepdims=True)
        staged[index] = meta[:META_USED]
        staged[index, 2:3, :] = jnp.broadcast_to(filled, (1, LANES)).astype(jnp.int32)
    copy = pltpu.make_async_copy(staged, held, sem)
    copy.start()
    copy.wait()


def add_tiles(groups, first, per_group, held, panel_ref, total):
    feat = panel_ref.shape[1]
    for index, group in enumerate(groups):
        start = (first + index) * per_group
        filled = held[index, 2, 0]

        @pl.loop(0, (filled + UNROLL - 1) // UNROLL)
        def _(step):
            for one in range(UNROLL):
                slot = step * UNROLL + one
                tile_row, tile_col = held[index, 0, start + slot], held[index, 1, start + slot]
                tile = group[pl.ds(pl.multiple_of(slot * HALF, HALF), HALF), :]
                tile = jnp.where(slot < filled, tile, jnp.zeros_like(tile))
                block = panel_ref[pl.ds(pl.multiple_of(tile_col * TB, TB), TB), :]
                product = jnp.dot(tile, side_by_side(block), preferred_element_type=jnp.float32)
                rows = pl.ds(pl.multiple_of(tile_row * HALF, HALF), HALF)
                total[rows, : 2 * feat] += product
                total[rows, 2 * feat :] += tile.astype(jnp.float32)


def own_kernel(per_group, self_ref, features_ref, degree_ref, group, panel_ref, total, staged, held, sem):
    feat = panel_ref.shape[1]
    places([group], 0, per_group, staged, held, sem)
    scale = lax.rsqrt(1.0 + degree_ref[...].astype(jnp.float32)).T
    for part in range(degree_ref.shape[0]):
        rows = slice(part * LANES, (part + 1) * LANES)
        block = features_ref[rows, :].astype(jnp.float32) * scale[:, part : part + 1]
        panel_ref[rows, :] = block.astype(panel_ref.dtype)
    total[...] = jnp.zeros_like(total)

    @pl.when(self_ref[0] > 0)
    def _():
        at = lax.broadcasted_iota(jnp.int32, (HALF, LANES), 1)
        row = lax.broadcasted_iota(jnp.int32, (HALF, LANES), 0)
        same = (at % TB == 2 * row + at // TB).astype(jnp.float32).astype(jnp.bfloat16)

        @pl.loop(0, total.shape[0] // HALF // SELF_UNROLL)
        def _(first):
            for one in range(SELF_UNROLL):
                tile = first * SELF_UNROLL + one
                block = panel_ref[pl.ds(pl.multiple_of((self_ref[1] + tile) * TB, TB), TB), :]
                total[pl.ds(pl.multiple_of(tile * HALF, HALF), HALF), : 2 * feat] = jnp.dot(
                    same, side_by_side(block), preferred_element_type=jnp.float32
                )

    add_tiles([group], 0, per_group, held, panel_ref, total)


def moved_kernel(per_group, panel_ref, before_ref, *refs):
    groups, (out_ref, total, staged, held, sem) = refs[:-5], refs[-5:]
    feat = panel_ref.shape[1]
    places(groups, 1, per_group, staged, held, sem)
    total[...] = before_ref[...]
    add_tiles(groups, 1, per_group, held, panel_ref, total)
    out_rows = total.shape[0] // out_ref.shape[0]
    lane = lax.broadcasted_iota(jnp.int32, (META_ROWS, LANES), 1)
    line = lax.broadcasted_iota(jnp.int32, (META_ROWS, LANES), 0)
    half = (lane // TB == line % 2).astype(jnp.float32).astype(jnp.bfloat16)
    part = lax.broadcasted_iota(jnp.int32, (META_ROWS, out_rows), 0) // 2
    none = jnp.zeros((META_ROWS, out_ref.shape[2] - out_rows), jnp.float32)
    for device in range(out_ref.shape[0]):
        rows = slice(device * out_rows, (device + 1) * out_rows)
        out_ref[device, :out_rows, :] = total[rows, : 2 * feat].astype(out_ref.dtype)
        degree = sum(
            lax.dot_general(
                half, piece, (((1,), (1,)), ((), ())), preferred_element_type=jnp.float32
            )
            for piece in two_parts(total[rows, 2 * feat :])
        )
        high, low = (piece.astype(jnp.float32) for piece in two_parts(degree))
        lines = jnp.where(part == 0, high, jnp.where(part == 1, low, 0.0))
        out_ref[device, out_rows:, :] = jnp.concatenate([lines, none], axis=1).astype(out_ref.dtype)


def layer_kernel(node_total, arrived_ref, order_ref, weight_ref, cotangent_ref, act_ref, grad_ref):
    lines = arrived_ref.shape[1] - META_ROWS
    nodes, feat = cotangent_ref.shape
    total = arrived_ref[0].astype(jnp.float32)
    for device in range(1, arrived_ref.shape[0]):
        total += arrived_ref[device].astype(jnp.float32)
    diagonal = lax.broadcasted_iota(jnp.int32, (lines, lines), 0) == lax.broadcasted_iota(
        jnp.int32, (lines, lines), 1
    )
    normed = []
    for half in range(2):
        degrees = total[lines + half : lines + half + 1, :lines]
        degrees += total[lines + half + 2 : lines + half + 3, :lines]
        scale = jnp.where(diagonal, lax.rsqrt(1.0 + degrees), 0.0).sum(axis=1, keepdims=True)
        normed.append(total[:lines, half * feat : (half + 1) * feat] * scale)
    normed = jnp.concatenate(normed, axis=0).astype(jnp.bfloat16)
    line = lax.broadcasted_iota(jnp.int32, (nodes, nodes), 0)
    node = 2 * (line % lines) + line // lines
    chosen = (order_ref[...] == node).astype(jnp.float32).astype(jnp.bfloat16)
    over_rows = (((0,), (0,)), ((), ()))
    ordered = lax.dot_general(
        chosen, normed, over_rows, preferred_element_type=jnp.float32
    ).astype(jnp.bfloat16)
    pre = jnp.dot(ordered, weight_ref[...], preferred_element_type=jnp.float32)
    act_ref[...] = jnp.maximum(pre, 0.0).astype(act_ref.dtype)
    grad_ref[...] = (
        lax.dot_general(
            ordered, cotangent_ref[...], over_rows, preferred_element_type=jnp.float32
        )
        * node_total ** (-0.5)
    )


def packed_groups(coords, counts, values, step_total):
    tiles = values.shape[0]
    rows = tiles // step_total * HALF + META_ROWS
    return pl.pallas_call(
        pack_kernel,
        out_shape=[jax.ShapeDtypeStruct((rows, LANES), jnp.bfloat16)] * step_total,
        in_specs=[VMEM] * 3,
        out_specs=[VMEM] * step_total,
        scratch_shapes=[
            pltpu.VMEM((tiles * HALF, LANES), jnp.float32),
            pltpu.VMEM((META_ROWS, LANES), jnp.float32),
        ],
        compiler_params=PARAMS,
        name="pack",
    )(coords, counts, values)


def scratch_places(groups):
    shape = (groups, META_USED, LANES)
    return [pltpu.VMEM(shape, jnp.int32), pltpu.SMEM(shape, jnp.int32), pltpu.SemaphoreType.DMA]


def own_tiles(self_loop, features, source_degree, group, row_panel):
    panel_rows, feat = features.shape
    per_group = (group.shape[0] - META_ROWS) // HALF
    return pl.pallas_call(
        functools.partial(own_kernel, per_group),
        out_shape=[
            jax.ShapeDtypeStruct((panel_rows, feat), jnp.bfloat16),
            jax.ShapeDtypeStruct((row_panel // 2, 2 * feat + LANES), jnp.float32),
        ],
        in_specs=[SMEM] + [VMEM] * 3,
        out_specs=[VMEM] * 2,
        scratch_shapes=scratch_places(1),
        compiler_params=PARAMS,
        cost_estimate=pl.CostEstimate(
            flops=2 * 24 * TB * TB * feat * 8, bytes_accessed=6 * 1024 * 1024, transcendentals=0
        ),
        name="own_tiles",
    )(self_loop, features, source_degree.reshape(-1, LANES), group)


def moved_tiles(panel, before, groups, columns):
    per_group = (groups[0].shape[0] - META_ROWS) // HALF
    feat = panel.shape[1]
    return pl.pallas_call(
        functools.partial(moved_kernel, per_group),
        out_shape=jax.ShapeDtypeStruct(
            (columns, before.shape[0] // columns + META_ROWS, 2 * feat), jnp.bfloat16
        ),
        in_specs=[VMEM] * (2 + len(groups)),
        out_specs=VMEM,
        scratch_shapes=[pltpu.VMEM(before.shape, jnp.float32)] + scratch_places(len(groups)),
        compiler_params=PARAMS,
        name="moved_tiles",
    )(panel, before, *groups)


def layer(arrived, node_order, weight, cotangent, node_total):
    out_rows, feat = cotangent.shape
    return pl.pallas_call(
        functools.partial(layer_kernel, node_total),
        out_shape=(
            jax.ShapeDtypeStruct((out_rows, feat), jnp.bfloat16),
            jax.ShapeDtypeStruct((feat, feat), jnp.float32),
        ),
        in_specs=[VMEM] * 4,
        out_specs=(VMEM, VMEM),
        compiler_params=PARAMS,
        name="layer",
    )(arrived, node_order, weight, cotangent)


def per_device(
    features, source_degree, tile_coords, tile_counts, tile_values, weight, node_order, cotangent
):
    columns = lax.axis_size("col")
    row_count = lax.psum(1, ROW)
    step_total = min(4, columns)
    tiles = tile_counts.shape[-1]
    panel_rows, feat = features.shape
    out_rows = node_order.shape[-1]
    row_panel = out_rows * columns

    packed = packed_groups(
        tile_coords.reshape(2, tiles),
        tile_counts.reshape(1, tiles),
        tile_values.reshape(tiles, -1),
        step_total,
    )
    arriving = [passed_along(packed[step], "col", -step) for step in range(1, step_total)]
    row_index = lax.axis_index(ROW)
    holder = lax.axis_index("col") == row_index * columns // row_count
    self_start = row_index * row_panel % panel_rows // TB
    self_loop = jnp.stack([holder.astype(jnp.int32), self_start.astype(jnp.int32)])
    panel, before = own_tiles(self_loop, features, source_degree, packed[0], row_panel)
    outgoing = moved_tiles(panel, before, arriving, columns)
    arrived = exchanged(outgoing, "col")
    activations, local_grad = layer(
        arrived, node_order, weight, cotangent, out_rows * row_count * columns
    )
    share = exchanged(local_grad.reshape(lax.psum(1, PLANE), -1, feat), PLANE).sum(0)
    share = to_all(share, "z").sum(0)
    weight_grad = to_all(share, PLANE).reshape(local_grad.shape)
    return (activations, weight_grad)


def solution(mesh):
    rows, columns = mesh.devices.shape
    apart = Mesh(mesh.devices.reshape(2, rows // 2, columns), (*ROW, "col"))
    both = (*ROW, "col")
    in_specs = (
        P("col", None),
        P("col"),
        P(ROW, "col", None, None),
        P(ROW, "col", None),
        P(ROW, "col", None, None),
        P(),
        P(both, None),
        P(both, None),
    )
    out_specs = (P(both, None), P())
    return jax.shard_map(
        per_device, mesh=apart, in_specs=in_specs, out_specs=out_specs, check_vma=False
    )
```

```python
import functools

import jax
import jax.numpy as jnp
from jax import lax
from jax.experimental import pallas as pl
from jax.experimental.pallas import tpu as pltpu
from jax.sharding import Mesh, PartitionSpec as P

TB = 64
HALF = TB // 2
LANES = 2 * TB
META_ROWS = 16
META_USED = 8
UNROLL = 12
SELF_UNROLL = 8
ROW = ("x_hi", "z_hi", "z_lo")
PLANE = ("x_hi", "col")
VMEM = pl.BlockSpec(memory_space=pltpu.VMEM)
HBM = pl.BlockSpec(memory_space=pltpu.HBM)
SMEM = pl.BlockSpec(memory_space=pltpu.SMEM)
PARAMS = pltpu.CompilerParams(vmem_limit_bytes=32 * 1024 * 1024)
PACK_MIB = 62


def limit(mib):
    return pltpu.CompilerParams(vmem_limit_bytes=mib * 1024 * 1024)


def passed_along(value, axis, steps):
    count = lax.axis_size(axis)
    pairs = [(source, (source + steps) % count) for source in range(count)]
    return lax.ppermute(value, axis, pairs)


def exchanged(parts, axis):
    return lax.all_to_all(parts, axis, 0, 0)


def to_all(value, axis):
    count = lax.psum(1, axis)
    copies = jnp.broadcast_to(value[None], (count, *value.shape))
    return exchanged(lax.optimization_barrier(copies), axis)


def between(value, pairs):
    return lax.ppermute(value, "z_hi", pairs)


def is_group(*groups):
    here = lax.axis_index("z_hi")
    return functools.reduce(jnp.logical_or, [here == group for group in groups])


def summed_over_z(share):
    share = to_all(share, "z_lo").sum(0)
    joined = share + between(share, [(1, 2), (7, 6)])
    arrived = [between(joined, [(2, 0)]), between(joined, [(6, 0)])]
    arrived += [between(share, [(group, 0)]) for group in (3, 5, 4)]
    return sum(arrived, joined)


def spread_over_z(total):
    second, first, last = (between(total, [(0, group)]) for group in (2, 1, 7))
    total = jnp.where(is_group(2), second, total)
    total = jnp.where(is_group(1), first, jnp.where(is_group(7), last, total))
    total = jnp.where(is_group(3, 6), between(total, [(2, 3), (7, 6)]), total)
    return jnp.where(is_group(4, 5), between(total, [(3, 4), (6, 5)]), total)


def two_parts(value):
    high = value.astype(jnp.bfloat16)
    return high, (value - high.astype(jnp.float32)).astype(jnp.bfloat16)


def side_by_side(block):
    none = jnp.zeros_like(block)
    return jnp.concatenate(
        [jnp.concatenate([block, none], axis=1), jnp.concatenate([none, block], axis=1)], axis=0
    )


def spread(values_ref, wide, first):
    tiles = values_ref.shape[0]
    for chunk in range(HALF):
        piece = values_ref[:, chunk * LANES : (chunk + 1) * LANES].astype(jnp.float32)
        wide[pl.ds(first + chunk, tiles, stride=HALF), :] = piece


def pack_kernel(coords_hbm, counts_hbm, values_hbm, *refs):
    groups, (coords_ref, counts_ref, values_ref, wide, meta, sems) = refs[:-6], refs[-6:]
    count = len(groups)
    tiles = values_hbm.shape[0] // count
    rows = tiles * HALF
    copies = [
        pltpu.make_async_copy(
            values_hbm.at[pl.ds(index * tiles, tiles)], values_ref.at[index], sems.at[index]
        )
        for index in range(count)
    ]
    copies.append(pltpu.make_async_copy(coords_hbm, coords_ref, sems.at[count]))
    copies.append(pltpu.make_async_copy(counts_hbm, counts_ref, sems.at[count + 1]))
    for copy in copies:
        copy.start()
    meta[...] = jnp.zeros_like(meta)
    for index, group in enumerate(groups):
        copies[index].wait()
        spread(values_ref.at[index], wide, index * rows)
        group[:rows, :] = wide[index * rows : (index + 1) * rows, :].astype(group.dtype)
    copies[count].wait()
    copies[count + 1].wait()
    slots = counts_ref.shape[1]
    meta[0:2, :slots] = coords_ref[...].astype(jnp.float32)
    meta[2:3, :slots] = counts_ref[...].astype(jnp.float32)
    for group in groups:
        group[rows:, :] = meta[...].astype(group.dtype)


def places(groups, first, per_group, staged, held, sem):
    lane = lax.broadcasted_iota(jnp.int32, (1, LANES), 1)
    for index, group in enumerate(groups):
        meta = group[group.shape[0] - META_ROWS :, :].astype(jnp.float32).astype(jnp.int32)
        start = (first + index) * per_group
        own = (lane >= start) & (lane < start + per_group) & (meta[2:3, :] > 0)
        filled = own.astype(jnp.int32).astype(jnp.float32).sum(axis=1, keepdims=True)
        staged[index] = meta[:META_USED]
        staged[index, 2:3, :] = jnp.broadcast_to(filled, (1, LANES)).astype(jnp.int32)
    copy = pltpu.make_async_copy(staged, held, sem)
    copy.start()
    copy.wait()


def add_tiles(groups, first, per_group, held, panel_ref, total):
    feat = panel_ref.shape[1]
    for index, group in enumerate(groups):
        start = (first + index) * per_group
        filled = held[index, 2, 0]

        @pl.loop(0, (filled + UNROLL - 1) // UNROLL)
        def _(step):
            for one in range(UNROLL):
                slot = step * UNROLL + one
                tile_row, tile_col = held[index, 0, start + slot], held[index, 1, start + slot]
                tile = group[pl.ds(pl.multiple_of(slot * HALF, HALF), HALF), :]
                tile = jnp.where(slot < filled, tile, jnp.zeros_like(tile))
                block = panel_ref[pl.ds(pl.multiple_of(tile_col * TB, TB), TB), :]
                product = jnp.dot(tile, side_by_side(block), preferred_element_type=jnp.float32)
                rows = pl.ds(pl.multiple_of(tile_row * HALF, HALF), HALF)
                total[rows, : 2 * feat] += product
                total[rows, 2 * feat :] += tile.astype(jnp.float32)


def own_kernel(per_group, self_ref, features_ref, degree_ref, group, panel_ref, total, staged, held, sem):
    feat = panel_ref.shape[1]
    places([group], 0, per_group, staged, held, sem)
    scale = lax.rsqrt(1.0 + degree_ref[...].astype(jnp.float32)).T
    for part in range(degree_ref.shape[0]):
        rows = slice(part * LANES, (part + 1) * LANES)
        block = features_ref[rows, :].astype(jnp.float32) * scale[:, part : part + 1]
        panel_ref[rows, :] = block.astype(panel_ref.dtype)
    total[...] = jnp.zeros_like(total)

    @pl.when(self_ref[0] > 0)
    def _():
        at = lax.broadcasted_iota(jnp.int32, (HALF, LANES), 1)
        row = lax.broadcasted_iota(jnp.int32, (HALF, LANES), 0)
        same = (at % TB == 2 * row + at // TB).astype(jnp.float32).astype(jnp.bfloat16)

        @pl.loop(0, total.shape[0] // HALF // SELF_UNROLL)
        def _(first):
            for one in range(SELF_UNROLL):
                tile = first * SELF_UNROLL + one
                block = panel_ref[pl.ds(pl.multiple_of((self_ref[1] + tile) * TB, TB), TB), :]
                total[pl.ds(pl.multiple_of(tile * HALF, HALF), HALF), : 2 * feat] = jnp.dot(
                    same, side_by_side(block), preferred_element_type=jnp.float32
                )

    add_tiles([group], 0, per_group, held, panel_ref, total)


def moved_kernel(per_group, panel_ref, before_ref, *refs):
    groups, (out_ref, total, staged, held, sem) = refs[:-5], refs[-5:]
    feat = panel_ref.shape[1]
    places(groups, 1, per_group, staged, held, sem)
    total[...] = before_ref[...]
    add_tiles(groups, 1, per_group, held, panel_ref, total)
    out_rows = total.shape[0] // out_ref.shape[0]
    lane = lax.broadcasted_iota(jnp.int32, (META_ROWS, LANES), 1)
    line = lax.broadcasted_iota(jnp.int32, (META_ROWS, LANES), 0)
    half = (lane // TB == line % 2).astype(jnp.float32).astype(jnp.bfloat16)
    part = lax.broadcasted_iota(jnp.int32, (META_ROWS, out_rows), 0) // 2
    none = jnp.zeros((META_ROWS, out_ref.shape[2] - out_rows), jnp.float32)
    for device in range(out_ref.shape[0]):
        rows = slice(device * out_rows, (device + 1) * out_rows)
        out_ref[device, :out_rows, :] = total[rows, : 2 * feat].astype(out_ref.dtype)
        degree = sum(
            lax.dot_general(
                half, piece, (((1,), (1,)), ((), ())), preferred_element_type=jnp.float32
            )
            for piece in two_parts(total[rows, 2 * feat :])
        )
        high, low = (piece.astype(jnp.float32) for piece in two_parts(degree))
        lines = jnp.where(part == 0, high, jnp.where(part == 1, low, 0.0))
        out_ref[device, out_rows:, :] = jnp.concatenate([lines, none], axis=1).astype(out_ref.dtype)


def layer_kernel(node_total, arrived_ref, order_ref, weight_ref, cotangent_ref, act_ref, grad_ref):
    lines = arrived_ref.shape[1] - META_ROWS
    nodes, feat = cotangent_ref.shape
    total = arrived_ref[0].astype(jnp.float32)
    for device in range(1, arrived_ref.shape[0]):
        total += arrived_ref[device].astype(jnp.float32)
    diagonal = lax.broadcasted_iota(jnp.int32, (lines, lines), 0) == lax.broadcasted_iota(
        jnp.int32, (lines, lines), 1
    )
    normed = []
    for half in range(2):
        degrees = total[lines + half : lines + half + 1, :lines]
        degrees += total[lines + half + 2 : lines + half + 3, :lines]
        scale = jnp.where(diagonal, lax.rsqrt(1.0 + degrees), 0.0).sum(axis=1, keepdims=True)
        normed.append(total[:lines, half * feat : (half + 1) * feat] * scale)
    normed = jnp.concatenate(normed, axis=0).astype(jnp.bfloat16)
    line = lax.broadcasted_iota(jnp.int32, (nodes, nodes), 0)
    node = 2 * (line % lines) + line // lines
    chosen = (order_ref[...] == node).astype(jnp.float32).astype(jnp.bfloat16)
    over_rows = (((0,), (0,)), ((), ()))
    ordered = lax.dot_general(
        chosen, normed, over_rows, preferred_element_type=jnp.float32
    ).astype(jnp.bfloat16)
    pre = jnp.dot(ordered, weight_ref[...], preferred_element_type=jnp.float32)
    act_ref[...] = jnp.maximum(pre, 0.0).astype(act_ref.dtype)
    grad_ref[...] = (
        lax.dot_general(
            ordered, cotangent_ref[...], over_rows, preferred_element_type=jnp.float32
        )
        * node_total ** (-0.5)
    )


def packed_groups(coords, counts, values, step_total):
    per_group = values.shape[0] // step_total
    rows = per_group * HALF
    return pl.pallas_call(
        pack_kernel,
        out_shape=[jax.ShapeDtypeStruct((rows + META_ROWS, LANES), jnp.bfloat16)] * step_total,
        in_specs=[HBM] * 3,
        out_specs=[VMEM] * step_total,
        scratch_shapes=[
            pltpu.VMEM(coords.shape, jnp.int32),
            pltpu.VMEM(counts.shape, jnp.int32),
            pltpu.VMEM((step_total, per_group, values.shape[1]), jnp.bfloat16),
            pltpu.VMEM((step_total * rows, LANES), jnp.float32),
            pltpu.VMEM((META_ROWS, LANES), jnp.float32),
            pltpu.SemaphoreType.DMA((step_total + 2,)),
        ],
        compiler_params=limit(PACK_MIB),
        name="pack",
    )(coords, counts, values)


def scratch_places(groups):
    shape = (groups, META_USED, LANES)
    return [pltpu.VMEM(shape, jnp.int32), pltpu.SMEM(shape, jnp.int32), pltpu.SemaphoreType.DMA]


def own_tiles(self_loop, features, source_degree, group, row_panel):
    panel_rows, feat = features.shape
    per_group = (group.shape[0] - META_ROWS) // HALF
    return pl.pallas_call(
        functools.partial(own_kernel, per_group),
        out_shape=[
            jax.ShapeDtypeStruct((panel_rows, feat), jnp.bfloat16),
            jax.ShapeDtypeStruct((row_panel // 2, 2 * feat + LANES), jnp.float32),
        ],
        in_specs=[SMEM] + [VMEM] * 3,
        out_specs=[VMEM] * 2,
        scratch_shapes=scratch_places(1),
        compiler_params=PARAMS,
        cost_estimate=pl.CostEstimate(
            flops=2 * 24 * TB * TB * feat * 8, bytes_accessed=6 * 1024 * 1024, transcendentals=0
        ),
        name="own_tiles",
    )(self_loop, features, source_degree.reshape(-1, LANES), group)


def moved_tiles(panel, before, groups, columns):
    per_group = (groups[0].shape[0] - META_ROWS) // HALF
    feat = panel.shape[1]
    return pl.pallas_call(
        functools.partial(moved_kernel, per_group),
        out_shape=jax.ShapeDtypeStruct(
            (columns, before.shape[0] // columns + META_ROWS, 2 * feat), jnp.bfloat16
        ),
        in_specs=[VMEM] * (2 + len(groups)),
        out_specs=VMEM,
        scratch_shapes=[pltpu.VMEM(before.shape, jnp.float32)] + scratch_places(len(groups)),
        compiler_params=PARAMS,
        name="moved_tiles",
    )(panel, before, *groups)


def layer(arrived, node_order, weight, cotangent, node_total):
    out_rows, feat = cotangent.shape
    return pl.pallas_call(
        functools.partial(layer_kernel, node_total),
        out_shape=(
            jax.ShapeDtypeStruct((out_rows, feat), jnp.bfloat16),
            jax.ShapeDtypeStruct((feat, feat), jnp.float32),
        ),
        in_specs=[VMEM] * 4,
        out_specs=(VMEM, VMEM),
        compiler_params=PARAMS,
        name="layer",
    )(arrived, node_order, weight, cotangent)


def per_device(
    features, source_degree, tile_coords, tile_counts, tile_values, weight, node_order, cotangent
):
    columns = lax.axis_size("col")
    row_count = lax.psum(1, ROW)
    step_total = min(4, columns)
    tiles = tile_counts.shape[-1]
    panel_rows, feat = features.shape
    out_rows = node_order.shape[-1]
    row_panel = out_rows * columns

    packed = packed_groups(
        tile_coords.reshape(2, tiles),
        tile_counts.reshape(1, tiles),
        tile_values.reshape(tiles, -1),
        step_total,
    )
    arriving = [passed_along(packed[step], "col", -step) for step in range(1, step_total)]
    row_index = lax.axis_index(ROW)
    holder = lax.axis_index("col") == row_index * columns // row_count
    self_start = row_index * row_panel % panel_rows // TB
    self_loop = jnp.stack([holder.astype(jnp.int32), self_start.astype(jnp.int32)])
    panel, before = own_tiles(self_loop, features, source_degree, packed[0], row_panel)
    outgoing = moved_tiles(panel, before, arriving, columns)
    arrived = exchanged(outgoing, "col")
    activations, local_grad = layer(
        arrived, node_order, weight, cotangent, out_rows * row_count * columns
    )
    share = exchanged(local_grad.reshape(lax.psum(1, PLANE), -1, feat), PLANE).sum(0)
    share = spread_over_z(summed_over_z(share))
    weight_grad = to_all(share, PLANE).reshape(local_grad.shape)
    return (activations, weight_grad)


def solution(mesh):
    rows, columns = mesh.devices.shape
    apart = Mesh(mesh.devices.reshape(2, 8, rows // 16, columns), (*ROW, "col"))
    both = (*ROW, "col")
    in_specs = (
        P("col", None),
        P("col"),
        P(ROW, "col", None, None),
        P(ROW, "col", None),
        P(ROW, "col", None, None),
        P(),
        P(both, None),
        P(both, None),
    )
    out_specs = (P(both, None), P())
    return jax.shard_map(
        per_device, mesh=apart, in_specs=in_specs, out_specs=out_specs, check_vma=False
    )
```

```python
import functools

import jax
import jax.numpy as jnp
from jax import lax
from jax.experimental import pallas as pl
from jax.experimental.pallas import tpu as pltpu
from jax.sharding import Mesh, PartitionSpec as P

TB = 64
HALF = TB // 2
LANES = 2 * TB
META_ROWS = 16
META_USED = 8
UNROLL = 12
SELF_UNROLL = 8
ROW = ("x_hi", "z_hi", "z_lo")
PLANE = ("x_hi", "col")
VMEM = pl.BlockSpec(memory_space=pltpu.VMEM)
HBM = pl.BlockSpec(memory_space=pltpu.HBM)
SMEM = pl.BlockSpec(memory_space=pltpu.SMEM)
PARAMS = pltpu.CompilerParams(vmem_limit_bytes=32 * 1024 * 1024)
PACK_MIB = 62


def limit(mib):
    return pltpu.CompilerParams(vmem_limit_bytes=mib * 1024 * 1024)


def passed_along(value, axis, steps):
    count = lax.axis_size(axis)
    pairs = [(source, (source + steps) % count) for source in range(count)]
    return lax.ppermute(value, axis, pairs)


def exchanged(parts, axis):
    return lax.all_to_all(parts, axis, 0, 0)


def to_all(value, axis):
    count = lax.psum(1, axis)
    copies = jnp.broadcast_to(value[None], (count, *value.shape))
    return exchanged(lax.optimization_barrier(copies), axis)


def between(value, pairs):
    return lax.ppermute(value, "z_hi", pairs)


def is_group(*groups):
    here = lax.axis_index("z_hi")
    return functools.reduce(jnp.logical_or, [here == group for group in groups])


def summed_over_z(share):
    share = to_all(share, "z_lo").sum(0)
    arrived = [between(share, [(group, 1)]) for group in (5, 4, 0)]
    joined = share + between(share, [(2, 3), (7, 6)])
    arrived += [between(joined, [(group, 1)]) for group in (6, 3)]
    return sum(arrived, joined)


def spread_over_z(total):
    to_0, to_2, to_7 = (between(total, [(1, group)]) for group in (0, 2, 7))
    total = jnp.where(is_group(7), to_7, jnp.where(is_group(0), to_0, jnp.where(is_group(2), to_2, total)))
    total = jnp.where(is_group(3, 6), between(total, [(2, 3), (7, 6)]), total)
    return jnp.where(is_group(4, 5), between(total, [(3, 4), (6, 5)]), total)


def two_parts(value):
    high = value.astype(jnp.bfloat16)
    return high, (value - high.astype(jnp.float32)).astype(jnp.bfloat16)


def side_by_side(block):
    none = jnp.zeros_like(block)
    return jnp.concatenate(
        [jnp.concatenate([block, none], axis=1), jnp.concatenate([none, block], axis=1)], axis=0
    )


def spread(values_ref, wide, first):
    tiles = values_ref.shape[0]
    for chunk in range(HALF):
        piece = values_ref[:, chunk * LANES : (chunk + 1) * LANES].astype(jnp.float32)
        wide[pl.ds(first + chunk, tiles, stride=HALF), :] = piece


def pack_kernel(coords_hbm, counts_hbm, values_hbm, *refs):
    groups, (coords_ref, counts_ref, values_ref, wide, meta, sems) = refs[:-6], refs[-6:]
    count = len(groups)
    tiles = values_hbm.shape[0] // count
    rows = tiles * HALF
    copies = [
        pltpu.make_async_copy(
            values_hbm.at[pl.ds(index * tiles, tiles)], values_ref.at[index], sems.at[index]
        )
        for index in range(count)
    ]
    copies.append(pltpu.make_async_copy(coords_hbm, coords_ref, sems.at[count]))
    copies.append(pltpu.make_async_copy(counts_hbm, counts_ref, sems.at[count + 1]))
    for copy in copies:
        copy.start()
    meta[...] = jnp.zeros_like(meta)
    for index, group in enumerate(groups):
        copies[index].wait()
        spread(values_ref.at[index], wide, index * rows)
        group[:rows, :] = wide[index * rows : (index + 1) * rows, :].astype(group.dtype)
    copies[count].wait()
    copies[count + 1].wait()
    slots = counts_ref.shape[1]
    meta[0:2, :slots] = coords_ref[...].astype(jnp.float32)
    meta[2:3, :slots] = counts_ref[...].astype(jnp.float32)
    for group in groups:
        group[rows:, :] = meta[...].astype(group.dtype)


def places(groups, first, per_group, staged, held, sem):
    lane = lax.broadcasted_iota(jnp.int32, (1, LANES), 1)
    for index, group in enumerate(groups):
        meta = group[group.shape[0] - META_ROWS :, :].astype(jnp.float32).astype(jnp.int32)
        start = (first + index) * per_group
        own = (lane >= start) & (lane < start + per_group) & (meta[2:3, :] > 0)
        filled = own.astype(jnp.int32).astype(jnp.float32).sum(axis=1, keepdims=True)
        staged[index] = meta[:META_USED]
        staged[index, 2:3, :] = jnp.broadcast_to(filled, (1, LANES)).astype(jnp.int32)
    copy = pltpu.make_async_copy(staged, held, sem)
    copy.start()
    copy.wait()


def add_tiles(groups, first, per_group, held, panel_ref, total):
    feat = panel_ref.shape[1]
    for index, group in enumerate(groups):
        start = (first + index) * per_group
        filled = held[index, 2, 0]

        @pl.loop(0, (filled + UNROLL - 1) // UNROLL)
        def _(step):
            for one in range(UNROLL):
                slot = step * UNROLL + one
                tile_row, tile_col = held[index, 0, start + slot], held[index, 1, start + slot]
                tile = group[pl.ds(pl.multiple_of(slot * HALF, HALF), HALF), :]
                tile = jnp.where(slot < filled, tile, jnp.zeros_like(tile))
                block = panel_ref[pl.ds(pl.multiple_of(tile_col * TB, TB), TB), :]
                product = jnp.dot(tile, side_by_side(block), preferred_element_type=jnp.float32)
                rows = pl.ds(pl.multiple_of(tile_row * HALF, HALF), HALF)
                total[rows, : 2 * feat] += product
                total[rows, 2 * feat :] += tile.astype(jnp.float32)


def own_kernel(per_group, self_ref, features_ref, degree_ref, group, panel_ref, total, staged, held, sem):
    feat = panel_ref.shape[1]
    places([group], 0, per_group, staged, held, sem)
    scale = lax.rsqrt(1.0 + degree_ref[...].astype(jnp.float32)).T
    for part in range(degree_ref.shape[0]):
        rows = slice(part * LANES, (part + 1) * LANES)
        block = features_ref[rows, :].astype(jnp.float32) * scale[:, part : part + 1]
        panel_ref[rows, :] = block.astype(panel_ref.dtype)
    total[...] = jnp.zeros_like(total)

    @pl.when(self_ref[0] > 0)
    def _():
        at = lax.broadcasted_iota(jnp.int32, (HALF, LANES), 1)
        row = lax.broadcasted_iota(jnp.int32, (HALF, LANES), 0)
        same = (at % TB == 2 * row + at // TB).astype(jnp.float32).astype(jnp.bfloat16)

        @pl.loop(0, total.shape[0] // HALF // SELF_UNROLL)
        def _(first):
            for one in range(SELF_UNROLL):
                tile = first * SELF_UNROLL + one
                block = panel_ref[pl.ds(pl.multiple_of((self_ref[1] + tile) * TB, TB), TB), :]
                total[pl.ds(pl.multiple_of(tile * HALF, HALF), HALF), : 2 * feat] = jnp.dot(
                    same, side_by_side(block), preferred_element_type=jnp.float32
                )

    add_tiles([group], 0, per_group, held, panel_ref, total)


def moved_kernel(per_group, panel_ref, before_ref, *refs):
    groups, (out_ref, total, staged, held, sem) = refs[:-5], refs[-5:]
    feat = panel_ref.shape[1]
    places(groups, 1, per_group, staged, held, sem)
    total[...] = before_ref[...]
    add_tiles(groups, 1, per_group, held, panel_ref, total)
    out_rows = total.shape[0] // out_ref.shape[0]
    lane = lax.broadcasted_iota(jnp.int32, (META_ROWS, LANES), 1)
    line = lax.broadcasted_iota(jnp.int32, (META_ROWS, LANES), 0)
    half = (lane // TB == line % 2).astype(jnp.float32).astype(jnp.bfloat16)
    part = lax.broadcasted_iota(jnp.int32, (META_ROWS, out_rows), 0) // 2
    none = jnp.zeros((META_ROWS, out_ref.shape[2] - out_rows), jnp.float32)
    for device in range(out_ref.shape[0]):
        rows = slice(device * out_rows, (device + 1) * out_rows)
        out_ref[device, :out_rows, :] = total[rows, : 2 * feat].astype(out_ref.dtype)
        degree = sum(
            lax.dot_general(
                half, piece, (((1,), (1,)), ((), ())), preferred_element_type=jnp.float32
            )
            for piece in two_parts(total[rows, 2 * feat :])
        )
        high, low = (piece.astype(jnp.float32) for piece in two_parts(degree))
        lines = jnp.where(part == 0, high, jnp.where(part == 1, low, 0.0))
        out_ref[device, out_rows:, :] = jnp.concatenate([lines, none], axis=1).astype(out_ref.dtype)


def layer_kernel(node_total, arrived_ref, order_ref, weight_ref, cotangent_ref, act_ref, grad_ref):
    lines = arrived_ref.shape[1] - META_ROWS
    nodes, feat = cotangent_ref.shape
    total = arrived_ref[0].astype(jnp.float32)
    for device in range(1, arrived_ref.shape[0]):
        total += arrived_ref[device].astype(jnp.float32)
    diagonal = lax.broadcasted_iota(jnp.int32, (lines, lines), 0) == lax.broadcasted_iota(
        jnp.int32, (lines, lines), 1
    )
    normed = []
    for half in range(2):
        degrees = total[lines + half : lines + half + 1, :lines]
        degrees += total[lines + half + 2 : lines + half + 3, :lines]
        scale = jnp.where(diagonal, lax.rsqrt(1.0 + degrees), 0.0).sum(axis=1, keepdims=True)
        normed.append(total[:lines, half * feat : (half + 1) * feat] * scale)
    normed = jnp.concatenate(normed, axis=0).astype(jnp.bfloat16)
    line = lax.broadcasted_iota(jnp.int32, (nodes, nodes), 0)
    node = 2 * (line % lines) + line // lines
    chosen = (order_ref[...] == node).astype(jnp.float32).astype(jnp.bfloat16)
    over_rows = (((0,), (0,)), ((), ()))
    ordered = lax.dot_general(
        chosen, normed, over_rows, preferred_element_type=jnp.float32
    ).astype(jnp.bfloat16)
    pre = jnp.dot(ordered, weight_ref[...], preferred_element_type=jnp.float32)
    act_ref[...] = jnp.maximum(pre, 0.0).astype(act_ref.dtype)
    grad_ref[...] = (
        lax.dot_general(
            ordered, cotangent_ref[...], over_rows, preferred_element_type=jnp.float32
        )
        * node_total ** (-0.5)
    )


def packed_groups(coords, counts, values, step_total):
    per_group = values.shape[0] // step_total
    rows = per_group * HALF
    return pl.pallas_call(
        pack_kernel,
        out_shape=[jax.ShapeDtypeStruct((rows + META_ROWS, LANES), jnp.bfloat16)] * step_total,
        in_specs=[HBM] * 3,
        out_specs=[VMEM] * step_total,
        scratch_shapes=[
            pltpu.VMEM(coords.shape, jnp.int32),
            pltpu.VMEM(counts.shape, jnp.int32),
            pltpu.VMEM((step_total, per_group, values.shape[1]), jnp.bfloat16),
            pltpu.VMEM((step_total * rows, LANES), jnp.float32),
            pltpu.VMEM((META_ROWS, LANES), jnp.float32),
            pltpu.SemaphoreType.DMA((step_total + 2,)),
        ],
        compiler_params=limit(PACK_MIB),
        name="pack",
    )(coords, counts, values)


def scratch_places(groups):
    shape = (groups, META_USED, LANES)
    return [pltpu.VMEM(shape, jnp.int32), pltpu.SMEM(shape, jnp.int32), pltpu.SemaphoreType.DMA]


def own_tiles(self_loop, features, source_degree, group, row_panel):
    panel_rows, feat = features.shape
    per_group = (group.shape[0] - META_ROWS) // HALF
    return pl.pallas_call(
        functools.partial(own_kernel, per_group),
        out_shape=[
            jax.ShapeDtypeStruct((panel_rows, feat), jnp.bfloat16),
            jax.ShapeDtypeStruct((row_panel // 2, 2 * feat + LANES), jnp.float32),
        ],
        in_specs=[SMEM] + [VMEM] * 3,
        out_specs=[VMEM] * 2,
        scratch_shapes=scratch_places(1),
        compiler_params=PARAMS,
        cost_estimate=pl.CostEstimate(
            flops=2 * 24 * TB * TB * feat * 8, bytes_accessed=6 * 1024 * 1024, transcendentals=0
        ),
        name="own_tiles",
    )(self_loop, features, source_degree.reshape(-1, LANES), group)


def moved_tiles(panel, before, groups, columns):
    per_group = (groups[0].shape[0] - META_ROWS) // HALF
    feat = panel.shape[1]
    return pl.pallas_call(
        functools.partial(moved_kernel, per_group),
        out_shape=jax.ShapeDtypeStruct(
            (columns, before.shape[0] // columns + META_ROWS, 2 * feat), jnp.bfloat16
        ),
        in_specs=[VMEM] * (2 + len(groups)),
        out_specs=VMEM,
        scratch_shapes=[pltpu.VMEM(before.shape, jnp.float32)] + scratch_places(len(groups)),
        compiler_params=PARAMS,
        name="moved_tiles",
    )(panel, before, *groups)


def layer(arrived, node_order, weight, cotangent, node_total):
    out_rows, feat = cotangent.shape
    return pl.pallas_call(
        functools.partial(layer_kernel, node_total),
        out_shape=(
            jax.ShapeDtypeStruct((out_rows, feat), jnp.bfloat16),
            jax.ShapeDtypeStruct((feat, feat), jnp.float32),
        ),
        in_specs=[VMEM] * 4,
        out_specs=(VMEM, VMEM),
        compiler_params=PARAMS,
        name="layer",
    )(arrived, node_order, weight, cotangent)


def per_device(
    features, source_degree, tile_coords, tile_counts, tile_values, weight, node_order, cotangent
):
    columns = lax.axis_size("col")
    row_count = lax.psum(1, ROW)
    step_total = min(4, columns)
    tiles = tile_counts.shape[-1]
    panel_rows, feat = features.shape
    out_rows = node_order.shape[-1]
    row_panel = out_rows * columns

    packed = packed_groups(
        tile_coords.reshape(2, tiles),
        tile_counts.reshape(1, tiles),
        tile_values.reshape(tiles, -1),
        step_total,
    )
    arriving = [passed_along(packed[step], "col", -step) for step in range(1, step_total)]
    row_index = lax.axis_index(ROW)
    holder = lax.axis_index("col") == row_index * columns // row_count
    self_start = row_index * row_panel % panel_rows // TB
    self_loop = jnp.stack([holder.astype(jnp.int32), self_start.astype(jnp.int32)])
    panel, before = own_tiles(self_loop, features, source_degree, packed[0], row_panel)
    outgoing = moved_tiles(panel, before, arriving, columns)
    arrived = exchanged(outgoing, "col")
    activations, local_grad = layer(
        arrived, node_order, weight, cotangent, out_rows * row_count * columns
    )
    share = exchanged(local_grad.reshape(lax.psum(1, PLANE), -1, feat), PLANE).sum(0)
    share = spread_over_z(summed_over_z(share))
    weight_grad = to_all(share, PLANE).reshape(local_grad.shape)
    return (activations, weight_grad)


def solution(mesh):
    rows, columns = mesh.devices.shape
    apart = Mesh(mesh.devices.reshape(2, 8, rows // 16, columns), (*ROW, "col"))
    both = (*ROW, "col")
    in_specs = (
        P("col", None),
        P("col"),
        P(ROW, "col", None, None),
        P(ROW, "col", None),
        P(ROW, "col", None, None),
        P(),
        P(both, None),
        P(both, None),
    )
    out_specs = (P(both, None), P())
    return jax.shard_map(
        per_device, mesh=apart, in_specs=in_specs, out_specs=out_specs, check_vma=False
    )
```

```python
import functools

import jax
import jax.numpy as jnp
from jax import lax
from jax.experimental import pallas as pl
from jax.experimental.pallas import tpu as pltpu
from jax.sharding import Mesh, PartitionSpec as P

TB = 64
HALF = TB // 2
LANES = 2 * TB
META_ROWS = 16
META_USED = 8
UNROLL = 12
SELF_UNROLL = 8
ROW = ("x_hi", "z_hi", "z_lo")
PLANE = ("x_hi", "col")
VMEM = pl.BlockSpec(memory_space=pltpu.VMEM)
HBM = pl.BlockSpec(memory_space=pltpu.HBM)
SMEM = pl.BlockSpec(memory_space=pltpu.SMEM)
PARAMS = pltpu.CompilerParams(vmem_limit_bytes=32 * 1024 * 1024)
PACK_MIB = 62


def limit(mib):
    return pltpu.CompilerParams(vmem_limit_bytes=mib * 1024 * 1024)


def passed_along(value, axis, steps):
    count = lax.axis_size(axis)
    pairs = [(source, (source + steps) % count) for source in range(count)]
    return lax.ppermute(value, axis, pairs)


def exchanged(parts, axis):
    return lax.all_to_all(parts, axis, 0, 0)


def to_all(value, axis):
    count = lax.psum(1, axis)
    copies = jnp.broadcast_to(value[None], (count, *value.shape))
    return exchanged(lax.optimization_barrier(copies), axis)


def between(value, pairs):
    return lax.ppermute(value, "z_hi", pairs)


def is_group(*groups):
    here = lax.axis_index("z_hi")
    return functools.reduce(jnp.logical_or, [here == group for group in groups])


def summed_over_z(share):
    share = to_all(share, "z_lo").sum(0)
    arrived = [between(share, [(group, 0)]) for group in (4, 5, 3)]
    joined = share + between(share, [(1, 2), (7, 6)])
    arrived += [between(joined, [(group, 0)]) for group in (6, 2)]
    return sum(arrived, joined)


def spread_over_z(total):
    second, first, last = (between(total, [(0, group)]) for group in (2, 1, 7))
    total = jnp.where(
        is_group(7), last, jnp.where(is_group(1), first, jnp.where(is_group(2), second, total))
    )
    total = jnp.where(is_group(3, 6), between(total, [(2, 3), (7, 6)]), total)
    return jnp.where(is_group(4, 5), between(total, [(3, 4), (6, 5)]), total)


def two_parts(value):
    high = value.astype(jnp.bfloat16)
    return high, (value - high.astype(jnp.float32)).astype(jnp.bfloat16)


def side_by_side(block):
    none = jnp.zeros_like(block)
    return jnp.concatenate(
        [jnp.concatenate([block, none], axis=1), jnp.concatenate([none, block], axis=1)], axis=0
    )


def spread(values_ref, wide, first):
    tiles = values_ref.shape[0]
    for chunk in range(HALF):
        piece = values_ref[:, chunk * LANES : (chunk + 1) * LANES].astype(jnp.float32)
        wide[pl.ds(first + chunk, tiles, stride=HALF), :] = piece


def pack_kernel(coords_hbm, counts_hbm, values_hbm, *refs):
    groups, (coords_ref, counts_ref, values_ref, wide, meta, sems) = refs[:-6], refs[-6:]
    count = len(groups)
    tiles = values_hbm.shape[0] // count
    rows = tiles * HALF
    copies = [
        pltpu.make_async_copy(
            values_hbm.at[pl.ds(index * tiles, tiles)], values_ref.at[index], sems.at[index]
        )
        for index in range(count)
    ]
    copies.append(pltpu.make_async_copy(coords_hbm, coords_ref, sems.at[count]))
    copies.append(pltpu.make_async_copy(counts_hbm, counts_ref, sems.at[count + 1]))
    for copy in copies:
        copy.start()
    meta[...] = jnp.zeros_like(meta)
    for index, group in enumerate(groups):
        copies[index].wait()
        spread(values_ref.at[index], wide, index * rows)
        group[:rows, :] = wide[index * rows : (index + 1) * rows, :].astype(group.dtype)
    copies[count].wait()
    copies[count + 1].wait()
    slots = counts_ref.shape[1]
    meta[0:2, :slots] = coords_ref[...].astype(jnp.float32)
    meta[2:3, :slots] = counts_ref[...].astype(jnp.float32)
    for group in groups:
        group[rows:, :] = meta[...].astype(group.dtype)


def places(groups, first, per_group, staged, held, sem):
    lane = lax.broadcasted_iota(jnp.int32, (1, LANES), 1)
    for index, group in enumerate(groups):
        meta = group[group.shape[0] - META_ROWS :, :].astype(jnp.float32).astype(jnp.int32)
        start = (first + index) * per_group
        own = (lane >= start) & (lane < start + per_group) & (meta[2:3, :] > 0)
        filled = own.astype(jnp.int32).astype(jnp.float32).sum(axis=1, keepdims=True)
        staged[index] = meta[:META_USED]
        staged[index, 2:3, :] = jnp.broadcast_to(filled, (1, LANES)).astype(jnp.int32)
    copy = pltpu.make_async_copy(staged, held, sem)
    copy.start()
    copy.wait()


def add_tiles(groups, first, per_group, held, panel_ref, total):
    feat = panel_ref.shape[1]
    for index, group in enumerate(groups):
        start = (first + index) * per_group
        filled = held[index, 2, 0]

        @pl.loop(0, (filled + UNROLL - 1) // UNROLL)
        def _(step):
            for one in range(UNROLL):
                slot = step * UNROLL + one
                tile_row, tile_col = held[index, 0, start + slot], held[index, 1, start + slot]
                tile = group[pl.ds(pl.multiple_of(slot * HALF, HALF), HALF), :]
                tile = jnp.where(slot < filled, tile, jnp.zeros_like(tile))
                block = panel_ref[pl.ds(pl.multiple_of(tile_col * TB, TB), TB), :]
                product = jnp.dot(tile, side_by_side(block), preferred_element_type=jnp.float32)
                rows = pl.ds(pl.multiple_of(tile_row * HALF, HALF), HALF)
                total[rows, : 2 * feat] += product
                total[rows, 2 * feat :] += tile.astype(jnp.float32)


def own_kernel(per_group, self_ref, features_ref, degree_ref, group, panel_ref, total, staged, held, sem):
    feat = panel_ref.shape[1]
    places([group], 0, per_group, staged, held, sem)
    scale = lax.rsqrt(1.0 + degree_ref[...].astype(jnp.float32)).T
    for part in range(degree_ref.shape[0]):
        rows = slice(part * LANES, (part + 1) * LANES)
        block = features_ref[rows, :].astype(jnp.float32) * scale[:, part : part + 1]
        panel_ref[rows, :] = block.astype(panel_ref.dtype)
    total[...] = jnp.zeros_like(total)

    @pl.when(self_ref[0] > 0)
    def _():
        at = lax.broadcasted_iota(jnp.int32, (HALF, LANES), 1)
        row = lax.broadcasted_iota(jnp.int32, (HALF, LANES), 0)
        same = (at % TB == 2 * row + at // TB).astype(jnp.float32).astype(jnp.bfloat16)

        @pl.loop(0, total.shape[0] // HALF // SELF_UNROLL)
        def _(first):
            for one in range(SELF_UNROLL):
                tile = first * SELF_UNROLL + one
                block = panel_ref[pl.ds(pl.multiple_of((self_ref[1] + tile) * TB, TB), TB), :]
                total[pl.ds(pl.multiple_of(tile * HALF, HALF), HALF), : 2 * feat] = jnp.dot(
                    same, side_by_side(block), preferred_element_type=jnp.float32
                )

    add_tiles([group], 0, per_group, held, panel_ref, total)


def moved_kernel(per_group, panel_ref, before_ref, *refs):
    groups, (out_ref, total, staged, held, sem) = refs[:-5], refs[-5:]
    feat = panel_ref.shape[1]
    places(groups, 1, per_group, staged, held, sem)
    total[...] = before_ref[...]
    add_tiles(groups, 1, per_group, held, panel_ref, total)
    out_rows = total.shape[0] // out_ref.shape[0]
    lane = lax.broadcasted_iota(jnp.int32, (META_ROWS, LANES), 1)
    line = lax.broadcasted_iota(jnp.int32, (META_ROWS, LANES), 0)
    half = (lane // TB == line % 2).astype(jnp.float32).astype(jnp.bfloat16)
    part = lax.broadcasted_iota(jnp.int32, (META_ROWS, out_rows), 0) // 2
    none = jnp.zeros((META_ROWS, out_ref.shape[2] - out_rows), jnp.float32)
    for device in range(out_ref.shape[0]):
        rows = slice(device * out_rows, (device + 1) * out_rows)
        out_ref[device, :out_rows, :] = total[rows, : 2 * feat].astype(out_ref.dtype)
        degree = sum(
            lax.dot_general(
                half, piece, (((1,), (1,)), ((), ())), preferred_element_type=jnp.float32
            )
            for piece in two_parts(total[rows, 2 * feat :])
        )
        high, low = (piece.astype(jnp.float32) for piece in two_parts(degree))
        lines = jnp.where(part == 0, high, jnp.where(part == 1, low, 0.0))
        out_ref[device, out_rows:, :] = jnp.concatenate([lines, none], axis=1).astype(out_ref.dtype)


def layer_kernel(node_total, arrived_ref, order_ref, weight_ref, cotangent_ref, act_ref, grad_ref):
    lines = arrived_ref.shape[1] - META_ROWS
    nodes, feat = cotangent_ref.shape
    total = arrived_ref[0].astype(jnp.float32)
    for device in range(1, arrived_ref.shape[0]):
        total += arrived_ref[device].astype(jnp.float32)
    diagonal = lax.broadcasted_iota(jnp.int32, (lines, lines), 0) == lax.broadcasted_iota(
        jnp.int32, (lines, lines), 1
    )
    normed = []
    for half in range(2):
        degrees = total[lines + half : lines + half + 1, :lines]
        degrees += total[lines + half + 2 : lines + half + 3, :lines]
        scale = jnp.where(diagonal, lax.rsqrt(1.0 + degrees), 0.0).sum(axis=1, keepdims=True)
        normed.append(total[:lines, half * feat : (half + 1) * feat] * scale)
    normed = jnp.concatenate(normed, axis=0).astype(jnp.bfloat16)
    line = lax.broadcasted_iota(jnp.int32, (nodes, nodes), 0)
    node = 2 * (line % lines) + line // lines
    chosen = (order_ref[...] == node).astype(jnp.float32).astype(jnp.bfloat16)
    over_rows = (((0,), (0,)), ((), ()))
    ordered = lax.dot_general(
        chosen, normed, over_rows, preferred_element_type=jnp.float32
    ).astype(jnp.bfloat16)
    pre = jnp.dot(ordered, weight_ref[...], preferred_element_type=jnp.float32)
    act_ref[...] = jnp.maximum(pre, 0.0).astype(act_ref.dtype)
    grad_ref[...] = (
        lax.dot_general(
            ordered, cotangent_ref[...], over_rows, preferred_element_type=jnp.float32
        )
        * node_total ** (-0.5)
    )


def packed_groups(coords, counts, values, step_total):
    per_group = values.shape[0] // step_total
    rows = per_group * HALF
    return pl.pallas_call(
        pack_kernel,
        out_shape=[jax.ShapeDtypeStruct((rows + META_ROWS, LANES), jnp.bfloat16)] * step_total,
        in_specs=[HBM] * 3,
        out_specs=[VMEM] * step_total,
        scratch_shapes=[
            pltpu.VMEM(coords.shape, jnp.int32),
            pltpu.VMEM(counts.shape, jnp.int32),
            pltpu.VMEM((step_total, per_group, values.shape[1]), jnp.bfloat16),
            pltpu.VMEM((step_total * rows, LANES), jnp.float32),
            pltpu.VMEM((META_ROWS, LANES), jnp.float32),
            pltpu.SemaphoreType.DMA((step_total + 2,)),
        ],
        compiler_params=limit(PACK_MIB),
        name="pack",
    )(coords, counts, values)


def scratch_places(groups):
    shape = (groups, META_USED, LANES)
    return [pltpu.VMEM(shape, jnp.int32), pltpu.SMEM(shape, jnp.int32), pltpu.SemaphoreType.DMA]


def own_tiles(self_loop, features, source_degree, group, row_panel):
    panel_rows, feat = features.shape
    per_group = (group.shape[0] - META_ROWS) // HALF
    return pl.pallas_call(
        functools.partial(own_kernel, per_group),
        out_shape=[
            jax.ShapeDtypeStruct((panel_rows, feat), jnp.bfloat16),
            jax.ShapeDtypeStruct((row_panel // 2, 2 * feat + LANES), jnp.float32),
        ],
        in_specs=[SMEM] + [VMEM] * 3,
        out_specs=[VMEM] * 2,
        scratch_shapes=scratch_places(1),
        compiler_params=PARAMS,
        cost_estimate=pl.CostEstimate(
            flops=2 * 24 * TB * TB * feat * 8, bytes_accessed=6 * 1024 * 1024, transcendentals=0
        ),
        name="own_tiles",
    )(self_loop, features, source_degree.reshape(-1, LANES), group)


def moved_tiles(panel, before, groups, columns):
    per_group = (groups[0].shape[0] - META_ROWS) // HALF
    feat = panel.shape[1]
    return pl.pallas_call(
        functools.partial(moved_kernel, per_group),
        out_shape=jax.ShapeDtypeStruct(
            (columns, before.shape[0] // columns + META_ROWS, 2 * feat), jnp.bfloat16
        ),
        in_specs=[VMEM] * (2 + len(groups)),
        out_specs=VMEM,
        scratch_shapes=[pltpu.VMEM(before.shape, jnp.float32)] + scratch_places(len(groups)),
        compiler_params=PARAMS,
        name="moved_tiles",
    )(panel, before, *groups)


def layer(arrived, node_order, weight, cotangent, node_total):
    out_rows, feat = cotangent.shape
    return pl.pallas_call(
        functools.partial(layer_kernel, node_total),
        out_shape=(
            jax.ShapeDtypeStruct((out_rows, feat), jnp.bfloat16),
            jax.ShapeDtypeStruct((feat, feat), jnp.float32),
        ),
        in_specs=[VMEM] * 4,
        out_specs=(VMEM, VMEM),
        compiler_params=PARAMS,
        name="layer",
    )(arrived, node_order, weight, cotangent)


def per_device(
    features, source_degree, tile_coords, tile_counts, tile_values, weight, node_order, cotangent
):
    columns = lax.axis_size("col")
    row_count = lax.psum(1, ROW)
    step_total = min(4, columns)
    tiles = tile_counts.shape[-1]
    panel_rows, feat = features.shape
    out_rows = node_order.shape[-1]
    row_panel = out_rows * columns

    packed = packed_groups(
        tile_coords.reshape(2, tiles),
        tile_counts.reshape(1, tiles),
        tile_values.reshape(tiles, -1),
        step_total,
    )
    arriving = [passed_along(packed[step], "col", -step) for step in range(1, step_total)]
    row_index = lax.axis_index(ROW)
    holder = lax.axis_index("col") == row_index * columns // row_count
    self_start = row_index * row_panel % panel_rows // TB
    self_loop = jnp.stack([holder.astype(jnp.int32), self_start.astype(jnp.int32)])
    panel, before = own_tiles(self_loop, features, source_degree, packed[0], row_panel)
    outgoing = moved_tiles(panel, before, arriving, columns)
    arrived = exchanged(outgoing, "col")
    activations, local_grad = layer(
        arrived, node_order, weight, cotangent, out_rows * row_count * columns
    )
    share = exchanged(local_grad.reshape(lax.psum(1, PLANE), -1, feat), PLANE).sum(0)
    share = spread_over_z(summed_over_z(share))
    weight_grad = to_all(share, PLANE).reshape(local_grad.shape)
    return (activations, weight_grad)


def solution(mesh):
    rows, columns = mesh.devices.shape
    apart = Mesh(mesh.devices.reshape(2, 8, rows // 16, columns), (*ROW, "col"))
    both = (*ROW, "col")
    in_specs = (
        P("col", None),
        P("col"),
        P(ROW, "col", None, None),
        P(ROW, "col", None),
        P(ROW, "col", None, None),
        P(),
        P(both, None),
        P(both, None),
    )
    out_specs = (P(both, None), P())
    return jax.shard_map(
        per_device, mesh=apart, in_specs=in_specs, out_specs=out_specs, check_vma=False
    )
```

```python
import functools

import jax
import jax.numpy as jnp
from jax import lax
from jax.experimental import pallas as pl
from jax.experimental.pallas import tpu as pltpu
from jax.sharding import Mesh, PartitionSpec as P

TB = 64
HALF = TB // 2
LANES = 2 * TB
META_ROWS = 16
META_USED = 8
UNROLL = 12
SELF_UNROLL = 8
ROW = ("x_hi", "z_hi", "z_lo")
NEAR = ("x_hi", "z_lo")
VMEM = pl.BlockSpec(memory_space=pltpu.VMEM)
HBM = pl.BlockSpec(memory_space=pltpu.HBM)
SMEM = pl.BlockSpec(memory_space=pltpu.SMEM)
PARAMS = pltpu.CompilerParams(vmem_limit_bytes=32 * 1024 * 1024)
PACK_MIB = 62


def limit(mib):
    return pltpu.CompilerParams(vmem_limit_bytes=mib * 1024 * 1024)


def passed_along(value, axis, steps):
    count = lax.axis_size(axis)
    pairs = [(source, (source + steps) % count) for source in range(count)]
    return lax.ppermute(value, axis, pairs)


def exchanged(parts, axis):
    return lax.all_to_all(parts, axis, 0, 0)


def to_all(value, axis):
    count = lax.psum(1, axis)
    copies = jnp.broadcast_to(value[None], (count, *value.shape))
    return exchanged(lax.optimization_barrier(copies), axis)


def between(value, pairs):
    return lax.ppermute(value, "z_hi", pairs)


def is_group(*groups):
    here = lax.axis_index("z_hi")
    return functools.reduce(jnp.logical_or, [here == group for group in groups])


def summed_over_z(share):
    share = to_all(share, NEAR).sum(0)
    arrived = [between(share, [(group, 0)]) for group in (4, 5, 3)]
    joined = share + between(share, [(1, 2), (7, 6)])
    arrived += [between(joined, [(group, 0)]) for group in (6, 2)]
    return sum(arrived, joined)


def spread_over_z(total):
    second, first, last = (between(total, [(0, group)]) for group in (2, 1, 7))
    total = jnp.where(
        is_group(7), last, jnp.where(is_group(1), first, jnp.where(is_group(2), second, total))
    )
    total = jnp.where(is_group(3, 6), between(total, [(2, 3), (7, 6)]), total)
    return jnp.where(is_group(4, 5), between(total, [(3, 4), (6, 5)]), total)


def two_parts(value):
    high = value.astype(jnp.bfloat16)
    return high, (value - high.astype(jnp.float32)).astype(jnp.bfloat16)


def side_by_side(block):
    none = jnp.zeros_like(block)
    return jnp.concatenate(
        [jnp.concatenate([block, none], axis=1), jnp.concatenate([none, block], axis=1)], axis=0
    )


def spread(values_ref, wide, first):
    tiles = values_ref.shape[0]
    for chunk in range(HALF):
        piece = values_ref[:, chunk * LANES : (chunk + 1) * LANES].astype(jnp.float32)
        wide[pl.ds(first + chunk, tiles, stride=HALF), :] = piece


def pack_kernel(coords_hbm, counts_hbm, values_hbm, *refs):
    groups, (coords_ref, counts_ref, values_ref, wide, meta, sems) = refs[:-6], refs[-6:]
    count = len(groups)
    tiles = values_hbm.shape[0] // count
    rows = tiles * HALF
    copies = [
        pltpu.make_async_copy(
            values_hbm.at[pl.ds(index * tiles, tiles)], values_ref.at[index], sems.at[index]
        )
        for index in range(count)
    ]
    copies.append(pltpu.make_async_copy(coords_hbm, coords_ref, sems.at[count]))
    copies.append(pltpu.make_async_copy(counts_hbm, counts_ref, sems.at[count + 1]))
    for copy in copies:
        copy.start()
    meta[...] = jnp.zeros_like(meta)
    for index, group in enumerate(groups):
        copies[index].wait()
        spread(values_ref.at[index], wide, index * rows)
        group[:rows, :] = wide[index * rows : (index + 1) * rows, :].astype(group.dtype)
    copies[count].wait()
    copies[count + 1].wait()
    slots = counts_ref.shape[1]
    meta[0:2, :slots] = coords_ref[...].astype(jnp.float32)
    meta[2:3, :slots] = counts_ref[...].astype(jnp.float32)
    for group in groups:
        group[rows:, :] = meta[...].astype(group.dtype)


def places(groups, first, per_group, staged, held, sem):
    lane = lax.broadcasted_iota(jnp.int32, (1, LANES), 1)
    for index, group in enumerate(groups):
        meta = group[group.shape[0] - META_ROWS :, :].astype(jnp.float32).astype(jnp.int32)
        start = (first + index) * per_group
        own = (lane >= start) & (lane < start + per_group) & (meta[2:3, :] > 0)
        filled = own.astype(jnp.int32).astype(jnp.float32).sum(axis=1, keepdims=True)
        staged[index] = meta[:META_USED]
        staged[index, 2:3, :] = jnp.broadcast_to(filled, (1, LANES)).astype(jnp.int32)
    copy = pltpu.make_async_copy(staged, held, sem)
    copy.start()
    copy.wait()


def add_tiles(groups, first, per_group, held, panel_ref, total):
    feat = panel_ref.shape[1]
    for index, group in enumerate(groups):
        start = (first + index) * per_group
        filled = held[index, 2, 0]

        @pl.loop(0, (filled + UNROLL - 1) // UNROLL)
        def _(step):
            for one in range(UNROLL):
                slot = step * UNROLL + one
                tile_row, tile_col = held[index, 0, start + slot], held[index, 1, start + slot]
                tile = group[pl.ds(pl.multiple_of(slot * HALF, HALF), HALF), :]
                tile = jnp.where(slot < filled, tile, jnp.zeros_like(tile))
                block = panel_ref[pl.ds(pl.multiple_of(tile_col * TB, TB), TB), :]
                product = jnp.dot(tile, side_by_side(block), preferred_element_type=jnp.float32)
                rows = pl.ds(pl.multiple_of(tile_row * HALF, HALF), HALF)
                total[rows, : 2 * feat] += product
                total[rows, 2 * feat :] += tile.astype(jnp.float32)


def own_kernel(per_group, self_ref, features_ref, degree_ref, group, panel_ref, total, staged, held, sem):
    feat = panel_ref.shape[1]
    places([group], 0, per_group, staged, held, sem)
    scale = lax.rsqrt(1.0 + degree_ref[...].astype(jnp.float32)).T
    for part in range(degree_ref.shape[0]):
        rows = slice(part * LANES, (part + 1) * LANES)
        block = features_ref[rows, :].astype(jnp.float32) * scale[:, part : part + 1]
        panel_ref[rows, :] = block.astype(panel_ref.dtype)
    total[...] = jnp.zeros_like(total)

    @pl.when(self_ref[0] > 0)
    def _():
        at = lax.broadcasted_iota(jnp.int32, (HALF, LANES), 1)
        row = lax.broadcasted_iota(jnp.int32, (HALF, LANES), 0)
        same = (at % TB == 2 * row + at // TB).astype(jnp.float32).astype(jnp.bfloat16)

        @pl.loop(0, total.shape[0] // HALF // SELF_UNROLL)
        def _(first):
            for one in range(SELF_UNROLL):
                tile = first * SELF_UNROLL + one
                block = panel_ref[pl.ds(pl.multiple_of((self_ref[1] + tile) * TB, TB), TB), :]
                total[pl.ds(pl.multiple_of(tile * HALF, HALF), HALF), : 2 * feat] = jnp.dot(
                    same, side_by_side(block), preferred_element_type=jnp.float32
                )

    add_tiles([group], 0, per_group, held, panel_ref, total)


def moved_kernel(per_group, panel_ref, before_ref, *refs):
    groups, (out_ref, total, staged, held, sem) = refs[:-5], refs[-5:]
    feat = panel_ref.shape[1]
    places(groups, 1, per_group, staged, held, sem)
    total[...] = before_ref[...]
    add_tiles(groups, 1, per_group, held, panel_ref, total)
    out_rows = total.shape[0] // out_ref.shape[0]
    lane = lax.broadcasted_iota(jnp.int32, (META_ROWS, LANES), 1)
    line = lax.broadcasted_iota(jnp.int32, (META_ROWS, LANES), 0)
    half = (lane // TB == line % 2).astype(jnp.float32).astype(jnp.bfloat16)
    part = lax.broadcasted_iota(jnp.int32, (META_ROWS, out_rows), 0) // 2
    none = jnp.zeros((META_ROWS, out_ref.shape[2] - out_rows), jnp.float32)
    for device in range(out_ref.shape[0]):
        rows = slice(device * out_rows, (device + 1) * out_rows)
        out_ref[device, :out_rows, :] = total[rows, : 2 * feat].astype(out_ref.dtype)
        degree = sum(
            lax.dot_general(
                half, piece, (((1,), (1,)), ((), ())), preferred_element_type=jnp.float32
            )
            for piece in two_parts(total[rows, 2 * feat :])
        )
        high, low = (piece.astype(jnp.float32) for piece in two_parts(degree))
        lines = jnp.where(part == 0, high, jnp.where(part == 1, low, 0.0))
        out_ref[device, out_rows:, :] = jnp.concatenate([lines, none], axis=1).astype(out_ref.dtype)


def layer_kernel(node_total, arrived_ref, order_ref, weight_ref, cotangent_ref, act_ref, grad_ref):
    lines = arrived_ref.shape[1] - META_ROWS
    nodes, feat = cotangent_ref.shape
    total = arrived_ref[0].astype(jnp.float32)
    for device in range(1, arrived_ref.shape[0]):
        total += arrived_ref[device].astype(jnp.float32)
    diagonal = lax.broadcasted_iota(jnp.int32, (lines, lines), 0) == lax.broadcasted_iota(
        jnp.int32, (lines, lines), 1
    )
    normed = []
    for half in range(2):
        degrees = total[lines + half : lines + half + 1, :lines]
        degrees += total[lines + half + 2 : lines + half + 3, :lines]
        scale = jnp.where(diagonal, lax.rsqrt(1.0 + degrees), 0.0).sum(axis=1, keepdims=True)
        normed.append(total[:lines, half * feat : (half + 1) * feat] * scale)
    normed = jnp.concatenate(normed, axis=0).astype(jnp.bfloat16)
    line = lax.broadcasted_iota(jnp.int32, (nodes, nodes), 0)
    node = 2 * (line % lines) + line // lines
    chosen = (order_ref[...] == node).astype(jnp.float32).astype(jnp.bfloat16)
    over_rows = (((0,), (0,)), ((), ()))
    ordered = lax.dot_general(
        chosen, normed, over_rows, preferred_element_type=jnp.float32
    ).astype(jnp.bfloat16)
    pre = jnp.dot(ordered, weight_ref[...], preferred_element_type=jnp.float32)
    act_ref[...] = jnp.maximum(pre, 0.0).astype(act_ref.dtype)
    grad_ref[...] = (
        lax.dot_general(
            ordered, cotangent_ref[...], over_rows, preferred_element_type=jnp.float32
        )
        * node_total ** (-0.5)
    )


def packed_groups(coords, counts, values, step_total):
    per_group = values.shape[0] // step_total
    rows = per_group * HALF
    return pl.pallas_call(
        pack_kernel,
        out_shape=[jax.ShapeDtypeStruct((rows + META_ROWS, LANES), jnp.bfloat16)] * step_total,
        in_specs=[HBM] * 3,
        out_specs=[VMEM] * step_total,
        scratch_shapes=[
            pltpu.VMEM(coords.shape, jnp.int32),
            pltpu.VMEM(counts.shape, jnp.int32),
            pltpu.VMEM((step_total, per_group, values.shape[1]), jnp.bfloat16),
            pltpu.VMEM((step_total * rows, LANES), jnp.float32),
            pltpu.VMEM((META_ROWS, LANES), jnp.float32),
            pltpu.SemaphoreType.DMA((step_total + 2,)),
        ],
        compiler_params=limit(PACK_MIB),
        name="pack",
    )(coords, counts, values)


def scratch_places(groups):
    shape = (groups, META_USED, LANES)
    return [pltpu.VMEM(shape, jnp.int32), pltpu.SMEM(shape, jnp.int32), pltpu.SemaphoreType.DMA]


def own_tiles(self_loop, features, source_degree, group, row_panel):
    panel_rows, feat = features.shape
    per_group = (group.shape[0] - META_ROWS) // HALF
    return pl.pallas_call(
        functools.partial(own_kernel, per_group),
        out_shape=[
            jax.ShapeDtypeStruct((panel_rows, feat), jnp.bfloat16),
            jax.ShapeDtypeStruct((row_panel // 2, 2 * feat + LANES), jnp.float32),
        ],
        in_specs=[SMEM] + [VMEM] * 3,
        out_specs=[VMEM] * 2,
        scratch_shapes=scratch_places(1),
        compiler_params=PARAMS,
        cost_estimate=pl.CostEstimate(
            flops=2 * 24 * TB * TB * feat * 8, bytes_accessed=6 * 1024 * 1024, transcendentals=0
        ),
        name="own_tiles",
    )(self_loop, features, source_degree.reshape(-1, LANES), group)


def moved_tiles(panel, before, groups, columns):
    per_group = (groups[0].shape[0] - META_ROWS) // HALF
    feat = panel.shape[1]
    return pl.pallas_call(
        functools.partial(moved_kernel, per_group),
        out_shape=jax.ShapeDtypeStruct(
            (columns, before.shape[0] // columns + META_ROWS, 2 * feat), jnp.bfloat16
        ),
        in_specs=[VMEM] * (2 + len(groups)),
        out_specs=VMEM,
        scratch_shapes=[pltpu.VMEM(before.shape, jnp.float32)] + scratch_places(len(groups)),
        compiler_params=PARAMS,
        name="moved_tiles",
    )(panel, before, *groups)


def layer(arrived, node_order, weight, cotangent, node_total):
    out_rows, feat = cotangent.shape
    return pl.pallas_call(
        functools.partial(layer_kernel, node_total),
        out_shape=(
            jax.ShapeDtypeStruct((out_rows, feat), jnp.bfloat16),
            jax.ShapeDtypeStruct((feat, feat), jnp.float32),
        ),
        in_specs=[VMEM] * 4,
        out_specs=(VMEM, VMEM),
        compiler_params=PARAMS,
        name="layer",
    )(arrived, node_order, weight, cotangent)


def per_device(
    features, source_degree, tile_coords, tile_counts, tile_values, weight, node_order, cotangent
):
    columns = lax.axis_size("col")
    row_count = lax.psum(1, ROW)
    step_total = min(4, columns)
    tiles = tile_counts.shape[-1]
    panel_rows, feat = features.shape
    out_rows = node_order.shape[-1]
    row_panel = out_rows * columns

    packed = packed_groups(
        tile_coords.reshape(2, tiles),
        tile_counts.reshape(1, tiles),
        tile_values.reshape(tiles, -1),
        step_total,
    )
    arriving = [passed_along(packed[step], "col", -step) for step in range(1, step_total)]
    row_index = lax.axis_index(ROW)
    holder = lax.axis_index("col") == row_index * columns // row_count
    self_start = row_index * row_panel % panel_rows // TB
    self_loop = jnp.stack([holder.astype(jnp.int32), self_start.astype(jnp.int32)])
    panel, before = own_tiles(self_loop, features, source_degree, packed[0], row_panel)
    outgoing = moved_tiles(panel, before, arriving, columns)
    arrived = exchanged(outgoing, "col")
    activations, local_grad = layer(
        arrived, node_order, weight, cotangent, out_rows * row_count * columns
    )
    share = exchanged(local_grad.reshape(columns, -1, feat), "col").sum(0)
    share = spread_over_z(summed_over_z(share))
    weight_grad = to_all(share, "col").reshape(local_grad.shape)
    return (activations, weight_grad)


def solution(mesh):
    rows, columns = mesh.devices.shape
    apart = Mesh(mesh.devices.reshape(2, 8, rows // 16, columns), (*ROW, "col"))
    both = (*ROW, "col")
    in_specs = (
        P("col", None),
        P("col"),
        P(ROW, "col", None, None),
        P(ROW, "col", None),
        P(ROW, "col", None, None),
        P(),
        P(both, None),
        P(both, None),
    )
    out_specs = (P(both, None), P())
    return jax.shard_map(
        per_device, mesh=apart, in_specs=in_specs, out_specs=out_specs, check_vma=False
    )
```

```python
import functools

import jax
import jax.numpy as jnp
from jax import lax
from jax.experimental import pallas as pl
from jax.experimental.pallas import tpu as pltpu
from jax.sharding import Mesh, PartitionSpec as P

TB = 64
HALF = TB // 2
LANES = 2 * TB
META_ROWS = 16
META_USED = 8
UNROLL = 12
SELF_UNROLL = 8
ROW = ("x_hi", "z_hi", "z_lo")
NEAR = ("x_hi", "z_lo")
VMEM = pl.BlockSpec(memory_space=pltpu.VMEM)
HBM = pl.BlockSpec(memory_space=pltpu.HBM)
SMEM = pl.BlockSpec(memory_space=pltpu.SMEM)
PARAMS = pltpu.CompilerParams(vmem_limit_bytes=32 * 1024 * 1024)
PACK_MIB = 62


def limit(mib):
    return pltpu.CompilerParams(vmem_limit_bytes=mib * 1024 * 1024)


def passed_along(value, axis, steps):
    count = lax.axis_size(axis)
    pairs = [(source, (source + steps) % count) for source in range(count)]
    return lax.ppermute(value, axis, pairs)


def exchanged(parts, axis):
    return lax.all_to_all(parts, axis, 0, 0)


def to_all(value, axis):
    count = lax.psum(1, axis)
    copies = jnp.broadcast_to(value[None], (count, *value.shape))
    return exchanged(lax.optimization_barrier(copies), axis)


def between(value, pairs):
    return lax.ppermute(value, "z_hi", pairs)


def is_group(*groups):
    here = lax.axis_index("z_hi")
    return functools.reduce(jnp.logical_or, [here == group for group in groups])


def summed_over_z(share):
    arrived = [between(share, [(group, 0)]) for group in (4, 5, 3)]
    joined = share + between(share, [(1, 2), (7, 6)])
    arrived += [between(joined, [(group, 0)]) for group in (6, 2)]
    return to_all(sum(arrived, joined), NEAR).sum(0)


def spread_over_z(total):
    second, first, last = (between(total, [(0, group)]) for group in (2, 1, 7))
    total = jnp.where(
        is_group(7), last, jnp.where(is_group(1), first, jnp.where(is_group(2), second, total))
    )
    total = jnp.where(is_group(3, 6), between(total, [(2, 3), (7, 6)]), total)
    return jnp.where(is_group(4, 5), between(total, [(3, 4), (6, 5)]), total)


def two_parts(value):
    high = value.astype(jnp.bfloat16)
    return high, (value - high.astype(jnp.float32)).astype(jnp.bfloat16)


def side_by_side(block):
    none = jnp.zeros_like(block)
    return jnp.concatenate(
        [jnp.concatenate([block, none], axis=1), jnp.concatenate([none, block], axis=1)], axis=0
    )


def spread(values_ref, wide, first):
    tiles = values_ref.shape[0]
    for chunk in range(HALF):
        piece = values_ref[:, chunk * LANES : (chunk + 1) * LANES].astype(jnp.float32)
        wide[pl.ds(first + chunk, tiles, stride=HALF), :] = piece


def pack_kernel(coords_hbm, counts_hbm, values_hbm, *refs):
    groups, (coords_ref, counts_ref, values_ref, wide, meta, sems) = refs[:-6], refs[-6:]
    count = len(groups)
    tiles = values_hbm.shape[0] // count
    rows = tiles * HALF
    copies = [
        pltpu.make_async_copy(
            values_hbm.at[pl.ds(index * tiles, tiles)], values_ref.at[index], sems.at[index]
        )
        for index in range(count)
    ]
    copies.append(pltpu.make_async_copy(coords_hbm, coords_ref, sems.at[count]))
    copies.append(pltpu.make_async_copy(counts_hbm, counts_ref, sems.at[count + 1]))
    for copy in copies:
        copy.start()
    meta[...] = jnp.zeros_like(meta)
    for index, group in enumerate(groups):
        copies[index].wait()
        spread(values_ref.at[index], wide, index * rows)
        group[:rows, :] = wide[index * rows : (index + 1) * rows, :].astype(group.dtype)
    copies[count].wait()
    copies[count + 1].wait()
    slots = counts_ref.shape[1]
    meta[0:2, :slots] = coords_ref[...].astype(jnp.float32)
    meta[2:3, :slots] = counts_ref[...].astype(jnp.float32)
    for group in groups:
        group[rows:, :] = meta[...].astype(group.dtype)


def places(groups, first, per_group, staged, held, sem):
    lane = lax.broadcasted_iota(jnp.int32, (1, LANES), 1)
    for index, group in enumerate(groups):
        meta = group[group.shape[0] - META_ROWS :, :].astype(jnp.float32).astype(jnp.int32)
        start = (first + index) * per_group
        own = (lane >= start) & (lane < start + per_group) & (meta[2:3, :] > 0)
        filled = own.astype(jnp.int32).astype(jnp.float32).sum(axis=1, keepdims=True)
        staged[index] = meta[:META_USED]
        staged[index, 2:3, :] = jnp.broadcast_to(filled, (1, LANES)).astype(jnp.int32)
    copy = pltpu.make_async_copy(staged, held, sem)
    copy.start()
    copy.wait()


def add_tiles(groups, first, per_group, held, panel_ref, total):
    feat = panel_ref.shape[1]
    for index, group in enumerate(groups):
        start = (first + index) * per_group
        filled = held[index, 2, 0]

        @pl.loop(0, (filled + UNROLL - 1) // UNROLL)
        def _(step):
            for one in range(UNROLL):
                slot = step * UNROLL + one
                tile_row, tile_col = held[index, 0, start + slot], held[index, 1, start + slot]
                tile = group[pl.ds(pl.multiple_of(slot * HALF, HALF), HALF), :]
                tile = jnp.where(slot < filled, tile, jnp.zeros_like(tile))
                block = panel_ref[pl.ds(pl.multiple_of(tile_col * TB, TB), TB), :]
                product = jnp.dot(tile, side_by_side(block), preferred_element_type=jnp.float32)
                rows = pl.ds(pl.multiple_of(tile_row * HALF, HALF), HALF)
                total[rows, : 2 * feat] += product
                total[rows, 2 * feat :] += tile.astype(jnp.float32)


def own_kernel(per_group, self_ref, features_ref, degree_ref, group, panel_ref, total, staged, held, sem):
    feat = panel_ref.shape[1]
    places([group], 0, per_group, staged, held, sem)
    scale = lax.rsqrt(1.0 + degree_ref[...].astype(jnp.float32)).T
    for part in range(degree_ref.shape[0]):
        rows = slice(part * LANES, (part + 1) * LANES)
        block = features_ref[rows, :].astype(jnp.float32) * scale[:, part : part + 1]
        panel_ref[rows, :] = block.astype(panel_ref.dtype)
    total[...] = jnp.zeros_like(total)

    @pl.when(self_ref[0] > 0)
    def _():
        at = lax.broadcasted_iota(jnp.int32, (HALF, LANES), 1)
        row = lax.broadcasted_iota(jnp.int32, (HALF, LANES), 0)
        same = (at % TB == 2 * row + at // TB).astype(jnp.float32).astype(jnp.bfloat16)

        @pl.loop(0, total.shape[0] // HALF // SELF_UNROLL)
        def _(first):
            for one in range(SELF_UNROLL):
                tile = first * SELF_UNROLL + one
                block = panel_ref[pl.ds(pl.multiple_of((self_ref[1] + tile) * TB, TB), TB), :]
                total[pl.ds(pl.multiple_of(tile * HALF, HALF), HALF), : 2 * feat] = jnp.dot(
                    same, side_by_side(block), preferred_element_type=jnp.float32
                )

    add_tiles([group], 0, per_group, held, panel_ref, total)


def moved_kernel(per_group, panel_ref, before_ref, *refs):
    groups, (out_ref, total, staged, held, sem) = refs[:-5], refs[-5:]
    feat = panel_ref.shape[1]
    places(groups, 1, per_group, staged, held, sem)
    total[...] = before_ref[...]
    add_tiles(groups, 1, per_group, held, panel_ref, total)
    out_rows = total.shape[0] // out_ref.shape[0]
    lane = lax.broadcasted_iota(jnp.int32, (META_ROWS, LANES), 1)
    line = lax.broadcasted_iota(jnp.int32, (META_ROWS, LANES), 0)
    half = (lane // TB == line % 2).astype(jnp.float32).astype(jnp.bfloat16)
    part = lax.broadcasted_iota(jnp.int32, (META_ROWS, out_rows), 0) // 2
    none = jnp.zeros((META_ROWS, out_ref.shape[2] - out_rows), jnp.float32)
    for device in range(out_ref.shape[0]):
        rows = slice(device * out_rows, (device + 1) * out_rows)
        out_ref[device, :out_rows, :] = total[rows, : 2 * feat].astype(out_ref.dtype)
        degree = sum(
            lax.dot_general(
                half, piece, (((1,), (1,)), ((), ())), preferred_element_type=jnp.float32
            )
            for piece in two_parts(total[rows, 2 * feat :])
        )
        high, low = (piece.astype(jnp.float32) for piece in two_parts(degree))
        lines = jnp.where(part == 0, high, jnp.where(part == 1, low, 0.0))
        out_ref[device, out_rows:, :] = jnp.concatenate([lines, none], axis=1).astype(out_ref.dtype)


def layer_kernel(node_total, arrived_ref, order_ref, weight_ref, cotangent_ref, act_ref, grad_ref):
    lines = arrived_ref.shape[1] - META_ROWS
    nodes, feat = cotangent_ref.shape
    total = arrived_ref[0].astype(jnp.float32)
    for device in range(1, arrived_ref.shape[0]):
        total += arrived_ref[device].astype(jnp.float32)
    diagonal = lax.broadcasted_iota(jnp.int32, (lines, lines), 0) == lax.broadcasted_iota(
        jnp.int32, (lines, lines), 1
    )
    normed = []
    for half in range(2):
        degrees = total[lines + half : lines + half + 1, :lines]
        degrees += total[lines + half + 2 : lines + half + 3, :lines]
        scale = jnp.where(diagonal, lax.rsqrt(1.0 + degrees), 0.0).sum(axis=1, keepdims=True)
        normed.append(total[:lines, half * feat : (half + 1) * feat] * scale)
    normed = jnp.concatenate(normed, axis=0).astype(jnp.bfloat16)
    line = lax.broadcasted_iota(jnp.int32, (nodes, nodes), 0)
    node = 2 * (line % lines) + line // lines
    chosen = (order_ref[...] == node).astype(jnp.float32).astype(jnp.bfloat16)
    over_rows = (((0,), (0,)), ((), ()))
    ordered = lax.dot_general(
        chosen, normed, over_rows, preferred_element_type=jnp.float32
    ).astype(jnp.bfloat16)
    pre = jnp.dot(ordered, weight_ref[...], preferred_element_type=jnp.float32)
    act_ref[...] = jnp.maximum(pre, 0.0).astype(act_ref.dtype)
    grad_ref[...] = (
        lax.dot_general(
            ordered, cotangent_ref[...], over_rows, preferred_element_type=jnp.float32
        )
        * node_total ** (-0.5)
    )


def packed_groups(coords, counts, values, step_total):
    per_group = values.shape[0] // step_total
    rows = per_group * HALF
    return pl.pallas_call(
        pack_kernel,
        out_shape=[jax.ShapeDtypeStruct((rows + META_ROWS, LANES), jnp.bfloat16)] * step_total,
        in_specs=[HBM] * 3,
        out_specs=[VMEM] * step_total,
        scratch_shapes=[
            pltpu.VMEM(coords.shape, jnp.int32),
            pltpu.VMEM(counts.shape, jnp.int32),
            pltpu.VMEM((step_total, per_group, values.shape[1]), jnp.bfloat16),
            pltpu.VMEM((step_total * rows, LANES), jnp.float32),
            pltpu.VMEM((META_ROWS, LANES), jnp.float32),
            pltpu.SemaphoreType.DMA((step_total + 2,)),
        ],
        compiler_params=limit(PACK_MIB),
        name="pack",
    )(coords, counts, values)


def scratch_places(groups):
    shape = (groups, META_USED, LANES)
    return [pltpu.VMEM(shape, jnp.int32), pltpu.SMEM(shape, jnp.int32), pltpu.SemaphoreType.DMA]


def own_tiles(self_loop, features, source_degree, group, row_panel):
    panel_rows, feat = features.shape
    per_group = (group.shape[0] - META_ROWS) // HALF
    return pl.pallas_call(
        functools.partial(own_kernel, per_group),
        out_shape=[
            jax.ShapeDtypeStruct((panel_rows, feat), jnp.bfloat16),
            jax.ShapeDtypeStruct((row_panel // 2, 2 * feat + LANES), jnp.float32),
        ],
        in_specs=[SMEM] + [VMEM] * 3,
        out_specs=[VMEM] * 2,
        scratch_shapes=scratch_places(1),
        compiler_params=PARAMS,
        cost_estimate=pl.CostEstimate(
            flops=2 * 24 * TB * TB * feat * 8, bytes_accessed=6 * 1024 * 1024, transcendentals=0
        ),
        name="own_tiles",
    )(self_loop, features, source_degree.reshape(-1, LANES), group)


def moved_tiles(panel, before, groups, columns):
    per_group = (groups[0].shape[0] - META_ROWS) // HALF
    feat = panel.shape[1]
    return pl.pallas_call(
        functools.partial(moved_kernel, per_group),
        out_shape=jax.ShapeDtypeStruct(
            (columns, before.shape[0] // columns + META_ROWS, 2 * feat), jnp.bfloat16
        ),
        in_specs=[VMEM] * (2 + len(groups)),
        out_specs=VMEM,
        scratch_shapes=[pltpu.VMEM(before.shape, jnp.float32)] + scratch_places(len(groups)),
        compiler_params=PARAMS,
        name="moved_tiles",
    )(panel, before, *groups)


def layer(arrived, node_order, weight, cotangent, node_total):
    out_rows, feat = cotangent.shape
    return pl.pallas_call(
        functools.partial(layer_kernel, node_total),
        out_shape=(
            jax.ShapeDtypeStruct((out_rows, feat), jnp.bfloat16),
            jax.ShapeDtypeStruct((feat, feat), jnp.float32),
        ),
        in_specs=[VMEM] * 4,
        out_specs=(VMEM, VMEM),
        compiler_params=PARAMS,
        name="layer",
    )(arrived, node_order, weight, cotangent)


def per_device(
    features, source_degree, tile_coords, tile_counts, tile_values, weight, node_order, cotangent
):
    columns = lax.axis_size("col")
    row_count = lax.psum(1, ROW)
    step_total = min(4, columns)
    tiles = tile_counts.shape[-1]
    panel_rows, feat = features.shape
    out_rows = node_order.shape[-1]
    row_panel = out_rows * columns

    packed = packed_groups(
        tile_coords.reshape(2, tiles),
        tile_counts.reshape(1, tiles),
        tile_values.reshape(tiles, -1),
        step_total,
    )
    arriving = [passed_along(packed[step], "col", -step) for step in range(1, step_total)]
    row_index = lax.axis_index(ROW)
    holder = lax.axis_index("col") == row_index * columns // row_count
    self_start = row_index * row_panel % panel_rows // TB
    self_loop = jnp.stack([holder.astype(jnp.int32), self_start.astype(jnp.int32)])
    panel, before = own_tiles(self_loop, features, source_degree, packed[0], row_panel)
    outgoing = moved_tiles(panel, before, arriving, columns)
    arrived = exchanged(outgoing, "col")
    activations, local_grad = layer(
        arrived, node_order, weight, cotangent, out_rows * row_count * columns
    )
    share = exchanged(local_grad.reshape(columns, -1, feat), "col").sum(0)
    share = spread_over_z(summed_over_z(share))
    weight_grad = to_all(share, "col").reshape(local_grad.shape)
    return (activations, weight_grad)


def solution(mesh):
    rows, columns = mesh.devices.shape
    apart = Mesh(mesh.devices.reshape(2, 8, rows // 16, columns), (*ROW, "col"))
    both = (*ROW, "col")
    in_specs = (
        P("col", None),
        P("col"),
        P(ROW, "col", None, None),
        P(ROW, "col", None),
        P(ROW, "col", None, None),
        P(),
        P(both, None),
        P(both, None),
    )
    out_specs = (P(both, None), P())
    return jax.shard_map(
        per_device, mesh=apart, in_specs=in_specs, out_specs=out_specs, check_vma=False
    )
```

```python
import functools

import jax
import jax.numpy as jnp
from jax import lax
from jax.experimental import pallas as pl
from jax.experimental.pallas import tpu as pltpu
from jax.sharding import Mesh, PartitionSpec as P

TB = 64
HALF = TB // 2
LANES = 2 * TB
META_ROWS = 16
META_USED = 8
UNROLL = 12
SELF_UNROLL = 8
ROW = ("x_hi", "z")
GROUPS, PLANES = 8, 4
VMEM = pl.BlockSpec(memory_space=pltpu.VMEM)
HBM = pl.BlockSpec(memory_space=pltpu.HBM)
SMEM = pl.BlockSpec(memory_space=pltpu.SMEM)
PARAMS = pltpu.CompilerParams(vmem_limit_bytes=32 * 1024 * 1024)
PACK_MIB = 62


def limit(mib):
    return pltpu.CompilerParams(vmem_limit_bytes=mib * 1024 * 1024)


def passed_along(value, axis, steps):
    count = lax.axis_size(axis)
    pairs = [(source, (source + steps) % count) for source in range(count)]
    return lax.ppermute(value, axis, pairs)


def exchanged(parts, axis):
    return lax.all_to_all(parts, axis, 0, 0)


def to_all(value, axis):
    count = lax.psum(1, axis)
    copies = jnp.broadcast_to(value[None], (count, *value.shape))
    return exchanged(lax.optimization_barrier(copies), axis)


def plane(group, place):
    return (1 + group * PLANES + place) % (GROUPS * PLANES)


def between(value, pairs):
    pairs = [(plane(a, place), plane(b, place)) for a, b in pairs for place in range(PLANES)]
    return lax.ppermute(value, "z", pairs)


def is_group(*groups):
    depth = GROUPS * PLANES
    here = (lax.axis_index("z") + depth - 1) % depth // PLANES
    return functools.reduce(jnp.logical_or, [here == group for group in groups])


def summed_in_group(value):
    depth = GROUPS * PLANES
    members = [
        [high * depth + plane(group, place) for high in range(2) for place in range(PLANES)]
        for group in range(GROUPS)
    ]
    copies = jnp.broadcast_to(value[None], (2 * PLANES, *value.shape))
    copies = lax.optimization_barrier(copies)
    return lax.all_to_all(copies, ROW, 0, 0, axis_index_groups=members).sum(0)


def summed_over_z(share):
    arrived = [between(share, [(group, 0)]) for group in (4, 5, 3)]
    joined = share + between(share, [(1, 2), (7, 6)])
    arrived += [between(joined, [(group, 0)]) for group in (6, 2)]
    return summed_in_group(sum(arrived, joined))


def spread_over_z(total):
    second, first, last = (between(total, [(0, group)]) for group in (2, 1, 7))
    total = jnp.where(
        is_group(2), second, jnp.where(is_group(7), last, jnp.where(is_group(1), first, total))
    )
    total = jnp.where(is_group(3, 6), between(total, [(2, 3), (7, 6)]), total)
    return jnp.where(is_group(4, 5), between(total, [(3, 4), (6, 5)]), total)


def two_parts(value):
    high = value.astype(jnp.bfloat16)
    return high, (value - high.astype(jnp.float32)).astype(jnp.bfloat16)


def side_by_side(block):
    none = jnp.zeros_like(block)
    return jnp.concatenate(
        [jnp.concatenate([block, none], axis=1), jnp.concatenate([none, block], axis=1)], axis=0
    )


def spread(values_ref, wide, first):
    tiles = values_ref.shape[0]
    for chunk in range(HALF):
        piece = values_ref[:, chunk * LANES : (chunk + 1) * LANES].astype(jnp.float32)
        wide[pl.ds(first + chunk, tiles, stride=HALF), :] = piece


def pack_kernel(coords_hbm, counts_hbm, values_hbm, *refs):
    groups, (coords_ref, counts_ref, values_ref, wide, meta, sems) = refs[:-6], refs[-6:]
    count = len(groups)
    tiles = values_hbm.shape[0] // count
    rows = tiles * HALF
    copies = [
        pltpu.make_async_copy(
            values_hbm.at[pl.ds(index * tiles, tiles)], values_ref.at[index], sems.at[index]
        )
        for index in range(count)
    ]
    copies.append(pltpu.make_async_copy(coords_hbm, coords_ref, sems.at[count]))
    copies.append(pltpu.make_async_copy(counts_hbm, counts_ref, sems.at[count + 1]))
    for copy in copies:
        copy.start()
    meta[...] = jnp.zeros_like(meta)
    for index, group in enumerate(groups):
        copies[index].wait()
        spread(values_ref.at[index], wide, index * rows)
        group[:rows, :] = wide[index * rows : (index + 1) * rows, :].astype(group.dtype)
    copies[count].wait()
    copies[count + 1].wait()
    slots = counts_ref.shape[1]
    meta[0:2, :slots] = coords_ref[...].astype(jnp.float32)
    meta[2:3, :slots] = counts_ref[...].astype(jnp.float32)
    for group in groups:
        group[rows:, :] = meta[...].astype(group.dtype)


def places(groups, first, per_group, staged, held, sem):
    lane = lax.broadcasted_iota(jnp.int32, (1, LANES), 1)
    for index, group in enumerate(groups):
        meta = group[group.shape[0] - META_ROWS :, :].astype(jnp.float32).astype(jnp.int32)
        start = (first + index) * per_group
        own = (lane >= start) & (lane < start + per_group) & (meta[2:3, :] > 0)
        filled = own.astype(jnp.int32).astype(jnp.float32).sum(axis=1, keepdims=True)
        staged[index] = meta[:META_USED]
        staged[index, 2:3, :] = jnp.broadcast_to(filled, (1, LANES)).astype(jnp.int32)
    copy = pltpu.make_async_copy(staged, held, sem)
    copy.start()
    copy.wait()


def add_tiles(groups, first, per_group, held, panel_ref, total):
    feat = panel_ref.shape[1]
    for index, group in enumerate(groups):
        start = (first + index) * per_group
        filled = held[index, 2, 0]

        @pl.loop(0, (filled + UNROLL - 1) // UNROLL)
        def _(step):
            for one in range(UNROLL):
                slot = step * UNROLL + one
                tile_row, tile_col = held[index, 0, start + slot], held[index, 1, start + slot]
                tile = group[pl.ds(pl.multiple_of(slot * HALF, HALF), HALF), :]
                tile = jnp.where(slot < filled, tile, jnp.zeros_like(tile))
                block = panel_ref[pl.ds(pl.multiple_of(tile_col * TB, TB), TB), :]
                product = jnp.dot(tile, side_by_side(block), preferred_element_type=jnp.float32)
                rows = pl.ds(pl.multiple_of(tile_row * HALF, HALF), HALF)
                total[rows, : 2 * feat] += product
                total[rows, 2 * feat :] += tile.astype(jnp.float32)


def own_kernel(per_group, self_ref, features_ref, degree_ref, group, panel_ref, total, staged, held, sem):
    feat = panel_ref.shape[1]
    places([group], 0, per_group, staged, held, sem)
    scale = lax.rsqrt(1.0 + degree_ref[...].astype(jnp.float32)).T
    for part in range(degree_ref.shape[0]):
        rows = slice(part * LANES, (part + 1) * LANES)
        block = features_ref[rows, :].astype(jnp.float32) * scale[:, part : part + 1]
        panel_ref[rows, :] = block.astype(panel_ref.dtype)
    total[...] = jnp.zeros_like(total)

    @pl.when(self_ref[0] > 0)
    def _():
        at = lax.broadcasted_iota(jnp.int32, (HALF, LANES), 1)
        row = lax.broadcasted_iota(jnp.int32, (HALF, LANES), 0)
        same = (at % TB == 2 * row + at // TB).astype(jnp.float32).astype(jnp.bfloat16)

        @pl.loop(0, total.shape[0] // HALF // SELF_UNROLL)
        def _(first):
            for one in range(SELF_UNROLL):
                tile = first * SELF_UNROLL + one
                block = panel_ref[pl.ds(pl.multiple_of((self_ref[1] + tile) * TB, TB), TB), :]
                total[pl.ds(pl.multiple_of(tile * HALF, HALF), HALF), : 2 * feat] = jnp.dot(
                    same, side_by_side(block), preferred_element_type=jnp.float32
                )

    add_tiles([group], 0, per_group, held, panel_ref, total)


def moved_kernel(per_group, panel_ref, before_ref, *refs):
    groups, (out_ref, total, staged, held, sem) = refs[:-5], refs[-5:]
    feat = panel_ref.shape[1]
    places(groups, 1, per_group, staged, held, sem)
    total[...] = before_ref[...]
    add_tiles(groups, 1, per_group, held, panel_ref, total)
    out_rows = total.shape[0] // out_ref.shape[0]
    lane = lax.broadcasted_iota(jnp.int32, (META_ROWS, LANES), 1)
    line = lax.broadcasted_iota(jnp.int32, (META_ROWS, LANES), 0)
    half = (lane // TB == line % 2).astype(jnp.float32).astype(jnp.bfloat16)
    part = lax.broadcasted_iota(jnp.int32, (META_ROWS, out_rows), 0) // 2
    none = jnp.zeros((META_ROWS, out_ref.shape[2] - out_rows), jnp.float32)
    for device in range(out_ref.shape[0]):
        rows = slice(device * out_rows, (device + 1) * out_rows)
        out_ref[device, :out_rows, :] = total[rows, : 2 * feat].astype(out_ref.dtype)
        degree = sum(
            lax.dot_general(
                half, piece, (((1,), (1,)), ((), ())), preferred_element_type=jnp.float32
            )
            for piece in two_parts(total[rows, 2 * feat :])
        )
        high, low = (piece.astype(jnp.float32) for piece in two_parts(degree))
        lines = jnp.where(part == 0, high, jnp.where(part == 1, low, 0.0))
        out_ref[device, out_rows:, :] = jnp.concatenate([lines, none], axis=1).astype(out_ref.dtype)


def layer_kernel(node_total, arrived_ref, order_ref, weight_ref, cotangent_ref, act_ref, grad_ref):
    lines = arrived_ref.shape[1] - META_ROWS
    nodes, feat = cotangent_ref.shape
    total = arrived_ref[0].astype(jnp.float32)
    for device in range(1, arrived_ref.shape[0]):
        total += arrived_ref[device].astype(jnp.float32)
    diagonal = lax.broadcasted_iota(jnp.int32, (lines, lines), 0) == lax.broadcasted_iota(
        jnp.int32, (lines, lines), 1
    )
    normed = []
    for half in range(2):
        degrees = total[lines + half : lines + half + 1, :lines]
        degrees += total[lines + half + 2 : lines + half + 3, :lines]
        scale = jnp.where(diagonal, lax.rsqrt(1.0 + degrees), 0.0).sum(axis=1, keepdims=True)
        normed.append(total[:lines, half * feat : (half + 1) * feat] * scale)
    normed = jnp.concatenate(normed, axis=0).astype(jnp.bfloat16)
    line = lax.broadcasted_iota(jnp.int32, (nodes, nodes), 0)
    node = 2 * (line % lines) + line // lines
    chosen = (order_ref[...] == node).astype(jnp.float32).astype(jnp.bfloat16)
    over_rows = (((0,), (0,)), ((), ()))
    ordered = lax.dot_general(
        chosen, normed, over_rows, preferred_element_type=jnp.float32
    ).astype(jnp.bfloat16)
    pre = jnp.dot(ordered, weight_ref[...], preferred_element_type=jnp.float32)
    act_ref[...] = jnp.maximum(pre, 0.0).astype(act_ref.dtype)
    grad_ref[...] = (
        lax.dot_general(
            ordered, cotangent_ref[...], over_rows, preferred_element_type=jnp.float32
        )
        * node_total ** (-0.5)
    )


def packed_groups(coords, counts, values, step_total):
    per_group = values.shape[0] // step_total
    rows = per_group * HALF
    return pl.pallas_call(
        pack_kernel,
        out_shape=[jax.ShapeDtypeStruct((rows + META_ROWS, LANES), jnp.bfloat16)] * step_total,
        in_specs=[HBM] * 3,
        out_specs=[VMEM] * step_total,
        scratch_shapes=[
            pltpu.VMEM(coords.shape, jnp.int32),
            pltpu.VMEM(counts.shape, jnp.int32),
            pltpu.VMEM((step_total, per_group, values.shape[1]), jnp.bfloat16),
            pltpu.VMEM((step_total * rows, LANES), jnp.float32),
            pltpu.VMEM((META_ROWS, LANES), jnp.float32),
            pltpu.SemaphoreType.DMA((step_total + 2,)),
        ],
        compiler_params=limit(PACK_MIB),
        name="pack",
    )(coords, counts, values)


def scratch_places(groups):
    shape = (groups, META_USED, LANES)
    return [pltpu.VMEM(shape, jnp.int32), pltpu.SMEM(shape, jnp.int32), pltpu.SemaphoreType.DMA]


def own_tiles(self_loop, features, source_degree, group, row_panel):
    panel_rows, feat = features.shape
    per_group = (group.shape[0] - META_ROWS) // HALF
    return pl.pallas_call(
        functools.partial(own_kernel, per_group),
        out_shape=[
            jax.ShapeDtypeStruct((panel_rows, feat), jnp.bfloat16),
            jax.ShapeDtypeStruct((row_panel // 2, 2 * feat + LANES), jnp.float32),
        ],
        in_specs=[SMEM] + [VMEM] * 3,
        out_specs=[VMEM] * 2,
        scratch_shapes=scratch_places(1),
        compiler_params=PARAMS,
        cost_estimate=pl.CostEstimate(
            flops=2 * 24 * TB * TB * feat * 8, bytes_accessed=6 * 1024 * 1024, transcendentals=0
        ),
        name="own_tiles",
    )(self_loop, features, source_degree.reshape(-1, LANES), group)


def moved_tiles(panel, before, groups, columns):
    per_group = (groups[0].shape[0] - META_ROWS) // HALF
    feat = panel.shape[1]
    return pl.pallas_call(
        functools.partial(moved_kernel, per_group),
        out_shape=jax.ShapeDtypeStruct(
            (columns, before.shape[0] // columns + META_ROWS, 2 * feat), jnp.bfloat16
        ),
        in_specs=[VMEM] * (2 + len(groups)),
        out_specs=VMEM,
        scratch_shapes=[pltpu.VMEM(before.shape, jnp.float32)] + scratch_places(len(groups)),
        compiler_params=PARAMS,
        name="moved_tiles",
    )(panel, before, *groups)


def layer(arrived, node_order, weight, cotangent, node_total):
    out_rows, feat = cotangent.shape
    return pl.pallas_call(
        functools.partial(layer_kernel, node_total),
        out_shape=(
            jax.ShapeDtypeStruct((out_rows, feat), jnp.bfloat16),
            jax.ShapeDtypeStruct((feat, feat), jnp.float32),
        ),
        in_specs=[VMEM] * 4,
        out_specs=(VMEM, VMEM),
        compiler_params=PARAMS,
        name="layer",
    )(arrived, node_order, weight, cotangent)


def per_device(
    features, source_degree, tile_coords, tile_counts, tile_values, weight, node_order, cotangent
):
    columns = lax.axis_size("col")
    row_count = lax.psum(1, ROW)
    step_total = min(4, columns)
    tiles = tile_counts.shape[-1]
    panel_rows, feat = features.shape
    out_rows = node_order.shape[-1]
    row_panel = out_rows * columns

    packed = packed_groups(
        tile_coords.reshape(2, tiles),
        tile_counts.reshape(1, tiles),
        tile_values.reshape(tiles, -1),
        step_total,
    )
    arriving = [passed_along(packed[step], "col", -step) for step in range(1, step_total)]
    row_index = lax.axis_index(ROW)
    holder = lax.axis_index("col") == row_index * columns // row_count
    self_start = row_index * row_panel % panel_rows // TB
    self_loop = jnp.stack([holder.astype(jnp.int32), self_start.astype(jnp.int32)])
    panel, before = own_tiles(self_loop, features, source_degree, packed[0], row_panel)
    outgoing = moved_tiles(panel, before, arriving, columns)
    arrived = exchanged(outgoing, "col")
    activations, local_grad = layer(
        arrived, node_order, weight, cotangent, out_rows * row_count * columns
    )
    share = exchanged(local_grad.reshape(columns, -1, feat), "col").sum(0)
    share = spread_over_z(summed_over_z(share))
    weight_grad = to_all(share, "col").reshape(local_grad.shape)
    return (activations, weight_grad)


def solution(mesh):
    rows, columns = mesh.devices.shape
    apart = Mesh(mesh.devices.reshape(2, rows // 2, columns), (*ROW, "col"))
    both = (*ROW, "col")
    in_specs = (
        P("col", None),
        P("col"),
        P(ROW, "col", None, None),
        P(ROW, "col", None),
        P(ROW, "col", None, None),
        P(),
        P(both, None),
        P(both, None),
    )
    out_specs = (P(both, None), P())
    return jax.shard_map(
        per_device, mesh=apart, in_specs=in_specs, out_specs=out_specs, check_vma=False
    )
```

```python
import functools

import jax
import jax.numpy as jnp
from jax import lax
from jax.experimental import pallas as pl
from jax.experimental.pallas import tpu as pltpu
from jax.sharding import Mesh, PartitionSpec as P

TB = 64
HALF = TB // 2
LANES = 2 * TB
META_ROWS = 16
META_USED = 8
UNROLL = 12
SELF_UNROLL = 8
ROW = ("x_hi", "z_hi", "z_lo")
NEAR = ("x_hi", "z_lo")
VMEM = pl.BlockSpec(memory_space=pltpu.VMEM)
HBM = pl.BlockSpec(memory_space=pltpu.HBM)
SMEM = pl.BlockSpec(memory_space=pltpu.SMEM)
PARAMS = pltpu.CompilerParams(vmem_limit_bytes=32 * 1024 * 1024)
PACK_MIB = 62


def limit(mib):
    return pltpu.CompilerParams(vmem_limit_bytes=mib * 1024 * 1024)


def passed_along(value, axis, steps):
    count = lax.axis_size(axis)
    pairs = [(source, (source + steps) % count) for source in range(count)]
    return lax.ppermute(value, axis, pairs)


def exchanged(parts, axis):
    return lax.all_to_all(parts, axis, 0, 0)


def to_all(value, axis):
    count = lax.psum(1, axis)
    copies = jnp.broadcast_to(value[None], (count, *value.shape))
    return exchanged(lax.optimization_barrier(copies), axis)


def between(value, pairs):
    return lax.ppermute(value, "z_hi", pairs)


def is_group(*groups):
    here = lax.axis_index("z_hi")
    return functools.reduce(jnp.logical_or, [here == group for group in groups])


def summed_over_z(share):
    arrived = [between(share, [(group, 0)]) for group in (4, 5, 3)]
    joined = share + between(share, [(1, 2), (7, 6)])
    arrived += [between(joined, [(group, 0)]) for group in (6, 2)]
    return to_all(sum(arrived, joined), NEAR).sum(0)


def spread_over_z(total):
    first, last = between(total, [(0, 1)]), between(total, [(0, 7)])
    total = jnp.where(is_group(1), first, jnp.where(is_group(7), last, total))
    far, near = between(total, [(1, 3), (7, 5)]), between(total, [(1, 2), (7, 6)])
    total = jnp.where(is_group(3, 5), far, jnp.where(is_group(2, 6), near, total))
    return jnp.where(is_group(4), between(total, [(3, 4)]), total)


def two_parts(value):
    high = value.astype(jnp.bfloat16)
    return high, (value - high.astype(jnp.float32)).astype(jnp.bfloat16)


def side_by_side(block):
    none = jnp.zeros_like(block)
    return jnp.concatenate(
        [jnp.concatenate([block, none], axis=1), jnp.concatenate([none, block], axis=1)], axis=0
    )


def spread(values_ref, wide, first):
    tiles = values_ref.shape[0]
    for chunk in range(HALF):
        piece = values_ref[:, chunk * LANES : (chunk + 1) * LANES].astype(jnp.float32)
        wide[pl.ds(first + chunk, tiles, stride=HALF), :] = piece


def pack_kernel(coords_hbm, counts_hbm, values_hbm, *refs):
    groups, (coords_ref, counts_ref, values_ref, wide, meta, sems) = refs[:-6], refs[-6:]
    count = len(groups)
    tiles = values_hbm.shape[0] // count
    rows = tiles * HALF
    copies = [
        pltpu.make_async_copy(
            values_hbm.at[pl.ds(index * tiles, tiles)], values_ref.at[index], sems.at[index]
        )
        for index in range(count)
    ]
    copies.append(pltpu.make_async_copy(coords_hbm, coords_ref, sems.at[count]))
    copies.append(pltpu.make_async_copy(counts_hbm, counts_ref, sems.at[count + 1]))
    for copy in copies:
        copy.start()
    meta[...] = jnp.zeros_like(meta)
    for index, group in enumerate(groups):
        copies[index].wait()
        spread(values_ref.at[index], wide, index * rows)
        group[:rows, :] = wide[index * rows : (index + 1) * rows, :].astype(group.dtype)
    copies[count].wait()
    copies[count + 1].wait()
    slots = counts_ref.shape[1]
    meta[0:2, :slots] = coords_ref[...].astype(jnp.float32)
    meta[2:3, :slots] = counts_ref[...].astype(jnp.float32)
    for group in groups:
        group[rows:, :] = meta[...].astype(group.dtype)


def places(groups, first, per_group, staged, held, sem):
    lane = lax.broadcasted_iota(jnp.int32, (1, LANES), 1)
    for index, group in enumerate(groups):
        meta = group[group.shape[0] - META_ROWS :, :].astype(jnp.float32).astype(jnp.int32)
        start = (first + index) * per_group
        own = (lane >= start) & (lane < start + per_group) & (meta[2:3, :] > 0)
        filled = own.astype(jnp.int32).astype(jnp.float32).sum(axis=1, keepdims=True)
        staged[index] = meta[:META_USED]
        staged[index, 2:3, :] = jnp.broadcast_to(filled, (1, LANES)).astype(jnp.int32)
    copy = pltpu.make_async_copy(staged, held, sem)
    copy.start()
    copy.wait()


def add_tiles(groups, first, per_group, held, panel_ref, total):
    feat = panel_ref.shape[1]
    for index, group in enumerate(groups):
        start = (first + index) * per_group
        filled = held[index, 2, 0]

        @pl.loop(0, (filled + UNROLL - 1) // UNROLL)
        def _(step):
            for one in range(UNROLL):
                slot = step * UNROLL + one
                tile_row, tile_col = held[index, 0, start + slot], held[index, 1, start + slot]
                tile = group[pl.ds(pl.multiple_of(slot * HALF, HALF), HALF), :]
                tile = jnp.where(slot < filled, tile, jnp.zeros_like(tile))
                block = panel_ref[pl.ds(pl.multiple_of(tile_col * TB, TB), TB), :]
                product = jnp.dot(tile, side_by_side(block), preferred_element_type=jnp.float32)
                rows = pl.ds(pl.multiple_of(tile_row * HALF, HALF), HALF)
                total[rows, : 2 * feat] += product
                total[rows, 2 * feat :] += tile.astype(jnp.float32)


def own_kernel(per_group, self_ref, features_ref, degree_ref, group, panel_ref, total, staged, held, sem):
    feat = panel_ref.shape[1]
    places([group], 0, per_group, staged, held, sem)
    scale = lax.rsqrt(1.0 + degree_ref[...].astype(jnp.float32)).T
    for part in range(degree_ref.shape[0]):
        rows = slice(part * LANES, (part + 1) * LANES)
        block = features_ref[rows, :].astype(jnp.float32) * scale[:, part : part + 1]
        panel_ref[rows, :] = block.astype(panel_ref.dtype)
    total[...] = jnp.zeros_like(total)

    @pl.when(self_ref[0] > 0)
    def _():
        at = lax.broadcasted_iota(jnp.int32, (HALF, LANES), 1)
        row = lax.broadcasted_iota(jnp.int32, (HALF, LANES), 0)
        same = (at % TB == 2 * row + at // TB).astype(jnp.float32).astype(jnp.bfloat16)

        @pl.loop(0, total.shape[0] // HALF // SELF_UNROLL)
        def _(first):
            for one in range(SELF_UNROLL):
                tile = first * SELF_UNROLL + one
                block = panel_ref[pl.ds(pl.multiple_of((self_ref[1] + tile) * TB, TB), TB), :]
                total[pl.ds(pl.multiple_of(tile * HALF, HALF), HALF), : 2 * feat] = jnp.dot(
                    same, side_by_side(block), preferred_element_type=jnp.float32
                )

    add_tiles([group], 0, per_group, held, panel_ref, total)


def moved_kernel(per_group, panel_ref, before_ref, *refs):
    groups, (out_ref, total, staged, held, sem) = refs[:-5], refs[-5:]
    feat = panel_ref.shape[1]
    places(groups, 1, per_group, staged, held, sem)
    total[...] = before_ref[...]
    add_tiles(groups, 1, per_group, held, panel_ref, total)
    out_rows = total.shape[0] // out_ref.shape[0]
    lane = lax.broadcasted_iota(jnp.int32, (META_ROWS, LANES), 1)
    line = lax.broadcasted_iota(jnp.int32, (META_ROWS, LANES), 0)
    half = (lane // TB == line % 2).astype(jnp.float32).astype(jnp.bfloat16)
    part = lax.broadcasted_iota(jnp.int32, (META_ROWS, out_rows), 0) // 2
    none = jnp.zeros((META_ROWS, out_ref.shape[2] - out_rows), jnp.float32)
    for device in range(out_ref.shape[0]):
        rows = slice(device * out_rows, (device + 1) * out_rows)
        out_ref[device, :out_rows, :] = total[rows, : 2 * feat].astype(out_ref.dtype)
        degree = sum(
            lax.dot_general(
                half, piece, (((1,), (1,)), ((), ())), preferred_element_type=jnp.float32
            )
            for piece in two_parts(total[rows, 2 * feat :])
        )
        high, low = (piece.astype(jnp.float32) for piece in two_parts(degree))
        lines = jnp.where(part == 0, high, jnp.where(part == 1, low, 0.0))
        out_ref[device, out_rows:, :] = jnp.concatenate([lines, none], axis=1).astype(out_ref.dtype)


def layer_kernel(node_total, arrived_ref, order_ref, weight_ref, cotangent_ref, act_ref, grad_ref):
    lines = arrived_ref.shape[1] - META_ROWS
    nodes, feat = cotangent_ref.shape
    total = arrived_ref[0].astype(jnp.float32)
    for device in range(1, arrived_ref.shape[0]):
        total += arrived_ref[device].astype(jnp.float32)
    diagonal = lax.broadcasted_iota(jnp.int32, (lines, lines), 0) == lax.broadcasted_iota(
        jnp.int32, (lines, lines), 1
    )
    normed = []
    for half in range(2):
        degrees = total[lines + half : lines + half + 1, :lines]
        degrees += total[lines + half + 2 : lines + half + 3, :lines]
        scale = jnp.where(diagonal, lax.rsqrt(1.0 + degrees), 0.0).sum(axis=1, keepdims=True)
        normed.append(total[:lines, half * feat : (half + 1) * feat] * scale)
    normed = jnp.concatenate(normed, axis=0).astype(jnp.bfloat16)
    line = lax.broadcasted_iota(jnp.int32, (nodes, nodes), 0)
    node = 2 * (line % lines) + line // lines
    chosen = (order_ref[...] == node).astype(jnp.float32).astype(jnp.bfloat16)
    over_rows = (((0,), (0,)), ((), ()))
    ordered = lax.dot_general(
        chosen, normed, over_rows, preferred_element_type=jnp.float32
    ).astype(jnp.bfloat16)
    pre = jnp.dot(ordered, weight_ref[...], preferred_element_type=jnp.float32)
    act_ref[...] = jnp.maximum(pre, 0.0).astype(act_ref.dtype)
    grad_ref[...] = (
        lax.dot_general(
            ordered, cotangent_ref[...], over_rows, preferred_element_type=jnp.float32
        )
        * node_total ** (-0.5)
    )


def packed_groups(coords, counts, values, step_total):
    per_group = values.shape[0] // step_total
    rows = per_group * HALF
    return pl.pallas_call(
        pack_kernel,
        out_shape=[jax.ShapeDtypeStruct((rows + META_ROWS, LANES), jnp.bfloat16)] * step_total,
        in_specs=[HBM] * 3,
        out_specs=[VMEM] * step_total,
        scratch_shapes=[
            pltpu.VMEM(coords.shape, jnp.int32),
            pltpu.VMEM(counts.shape, jnp.int32),
            pltpu.VMEM((step_total, per_group, values.shape[1]), jnp.bfloat16),
            pltpu.VMEM((step_total * rows, LANES), jnp.float32),
            pltpu.VMEM((META_ROWS, LANES), jnp.float32),
            pltpu.SemaphoreType.DMA((step_total + 2,)),
        ],
        compiler_params=limit(PACK_MIB),
        name="pack",
    )(coords, counts, values)


def scratch_places(groups):
    shape = (groups, META_USED, LANES)
    return [pltpu.VMEM(shape, jnp.int32), pltpu.SMEM(shape, jnp.int32), pltpu.SemaphoreType.DMA]


def own_tiles(self_loop, features, source_degree, group, row_panel):
    panel_rows, feat = features.shape
    per_group = (group.shape[0] - META_ROWS) // HALF
    return pl.pallas_call(
        functools.partial(own_kernel, per_group),
        out_shape=[
            jax.ShapeDtypeStruct((panel_rows, feat), jnp.bfloat16),
            jax.ShapeDtypeStruct((row_panel // 2, 2 * feat + LANES), jnp.float32),
        ],
        in_specs=[SMEM] + [VMEM] * 3,
        out_specs=[VMEM] * 2,
        scratch_shapes=scratch_places(1),
        compiler_params=PARAMS,
        cost_estimate=pl.CostEstimate(
            flops=2 * 24 * TB * TB * feat * 8, bytes_accessed=6 * 1024 * 1024, transcendentals=0
        ),
        name="own_tiles",
    )(self_loop, features, source_degree.reshape(-1, LANES), group)


def moved_tiles(panel, before, groups, columns):
    per_group = (groups[0].shape[0] - META_ROWS) // HALF
    feat = panel.shape[1]
    return pl.pallas_call(
        functools.partial(moved_kernel, per_group),
        out_shape=jax.ShapeDtypeStruct(
            (columns, before.shape[0] // columns + META_ROWS, 2 * feat), jnp.bfloat16
        ),
        in_specs=[VMEM] * (2 + len(groups)),
        out_specs=VMEM,
        scratch_shapes=[pltpu.VMEM(before.shape, jnp.float32)] + scratch_places(len(groups)),
        compiler_params=PARAMS,
        name="moved_tiles",
    )(panel, before, *groups)


def layer(arrived, node_order, weight, cotangent, node_total):
    out_rows, feat = cotangent.shape
    return pl.pallas_call(
        functools.partial(layer_kernel, node_total),
        out_shape=(
            jax.ShapeDtypeStruct((out_rows, feat), jnp.bfloat16),
            jax.ShapeDtypeStruct((feat, feat), jnp.float32),
        ),
        in_specs=[VMEM] * 4,
        out_specs=(VMEM, VMEM),
        compiler_params=PARAMS,
        name="layer",
    )(arrived, node_order, weight, cotangent)


def per_device(
    features, source_degree, tile_coords, tile_counts, tile_values, weight, node_order, cotangent
):
    columns = lax.axis_size("col")
    row_count = lax.psum(1, ROW)
    step_total = min(4, columns)
    tiles = tile_counts.shape[-1]
    panel_rows, feat = features.shape
    out_rows = node_order.shape[-1]
    row_panel = out_rows * columns

    packed = packed_groups(
        tile_coords.reshape(2, tiles),
        tile_counts.reshape(1, tiles),
        tile_values.reshape(tiles, -1),
        step_total,
    )
    arriving = [passed_along(packed[step], "col", -step) for step in range(1, step_total)]
    row_index = lax.axis_index(ROW)
    holder = lax.axis_index("col") == row_index * columns // row_count
    self_start = row_index * row_panel % panel_rows // TB
    self_loop = jnp.stack([holder.astype(jnp.int32), self_start.astype(jnp.int32)])
    panel, before = own_tiles(self_loop, features, source_degree, packed[0], row_panel)
    outgoing = moved_tiles(panel, before, arriving, columns)
    arrived = exchanged(outgoing, "col")
    activations, local_grad = layer(
        arrived, node_order, weight, cotangent, out_rows * row_count * columns
    )
    share = exchanged(local_grad.reshape(columns, -1, feat), "col").sum(0)
    share = spread_over_z(summed_over_z(share))
    weight_grad = to_all(share, "col").reshape(local_grad.shape)
    return (activations, weight_grad)


def solution(mesh):
    rows, columns = mesh.devices.shape
    apart = Mesh(mesh.devices.reshape(2, 8, rows // 16, columns), (*ROW, "col"))
    both = (*ROW, "col")
    in_specs = (
        P("col", None),
        P("col"),
        P(ROW, "col", None, None),
        P(ROW, "col", None),
        P(ROW, "col", None, None),
        P(),
        P(both, None),
        P(both, None),
    )
    out_specs = (P(both, None), P())
    return jax.shard_map(
        per_device, mesh=apart, in_specs=in_specs, out_specs=out_specs, check_vma=False
    )
```
